32 devices in a mesh: tm: 8 (over z, y), patch: 4 (over x, core).
Axes of the slice: x: 2, y: 2, z: 4, core: 2. Of those that a mesh axis runs over, the one named last changes fastest.
Arguments:
- latents: bfloat16 [1024, 1024], replicated, may hold values from -6 to 6
- tokens: bfloat16 [65536, 1024], P(('tm', 'patch')), may hold values from -300 to 300, as said below
- w_query: bfloat16 [1024, 1024], replicated, may hold values from -0.1875 to 0.1875
- w_key: bfloat16 [1024, 1024], replicated, may hold values from -0.1875 to 0.1875
- w_value: bfloat16 [1024, 1024], replicated, may hold values from -0.1875 to 0.1875
- w_out: bfloat16 [1024, 1024], P(None, 'patch'), may hold values from -0.1875 to 0.1875
Outputs:
- resampled: bfloat16 [1024, 1024], P('tm', 'patch')
The draws below stay inside these ranges and needn't reach their ends.
Inputs may be any that keep to these rules, and one draw needn't show every extreme that they name: `tokens`: token features; a few rows may be far larger than the rest.
All inputs are finite; a program needn't handle non-finite values.
Results may differ from the reference program's by a relative error of at most 0.006.
The reference program's roundings to bfloat16 on the way (of `query`, `weight` and `normed`) count: a program that leaves them out, or rounds other values in their place, can miss the bound.
Values may be sent and summed in bfloat16 or wider, within the bound.
No kernel may reach another device: no remote copies, remote signals or barrier semaphores. Data moves between devices by JAX's collectives and lax.ppermute only.
A program may use at most 192 MiB of HBM per device.

```python
import math
import jax
import jax.numpy as jnp
from jax import lax

D = 1024
H = 8
L = 1024
TOK_DEV = 2048
TOKENS = 65536
N_TM = 8
N_PATCH = 4


def draw_tokens(key, part):
    key = jax.random.fold_in(key, 11)
    first = jax.random.fold_in(key, 0)
    return jnp.clip(jax.random.normal(first, (TOKENS, D), jnp.float32), -6.0, 6.0).astype(jnp.bfloat16)


def block_scale(own_key, shape, pieces, smallest, top_value):
    loudness, own = 1.0, jax.random.fold_in(own_key, 6)
    for position, shards_of in pieces:
        steps = jnp.exp(jax.random.uniform(jax.random.fold_in(own, position), (shards_of,), jnp.float32, smallest / len(pieces), top_value / len(pieces)))
        loudness = loudness * jnp.repeat(steps, shape[position] // shards_of).reshape([-1 if axis == position else 1 for axis in range(len(shape))])
    return loudness


def bell_draw(own_key, shape, deviation, most, shards=(), held_as=jnp.bfloat16):
    entries = deviation * jax.random.normal(own_key, shape, jnp.float32)
    if shards:
        entries = entries * block_scale(own_key, shape, shards, -0.22, 0.18)
    return jnp.clip(entries, -most, most).astype(held_as)


def setup_inputs(seed: int = 0) -> dict:
    key_list = jax.random.split(jax.random.key(seed), 7)
    return {
        "latents": bell_draw(key_list[0], (L, D), 1.0, 6.0),
        "tokens": draw_tokens(jax.random.fold_in(key_list[6], 71), 0),
        "w_query": bell_draw(key_list[2], (D, D), D ** -0.5, 0.1875),
        "w_key": bell_draw(key_list[3], (D, D), D ** -0.5, 0.1875),
        "w_value": bell_draw(key_list[4], (D, D), D ** -0.5, 0.1875),
        "w_out": bell_draw(key_list[5], (D, D), D ** -0.5, 0.1875, ((1, 4),)),
    }


def block_part(query, block, w_key, w_value):
    head_size = D // H
    keys = jnp.dot(block, w_key, preferred_element_type=jnp.float32).astype(jnp.bfloat16)
    vals = jnp.dot(block, w_value, preferred_element_type=jnp.float32).astype(jnp.bfloat16)
    scale = 1.0 / math.sqrt(head_size)
    peaks, totals, parts = ([], [], [])
    for head in range(H):
        cols = slice(head * head_size, (head + 1) * head_size)
        score = jnp.dot(query[:, cols], keys[:, cols].T, preferred_element_type=jnp.float32) * scale
        top = lax.optimization_barrier(jnp.max(score, axis=1))
        weight = jnp.exp(score - top[:, None]).astype(jnp.bfloat16)
        peaks.append(top)
        totals.append(lax.optimization_barrier(jnp.sum(weight.astype(jnp.float32), axis=1)))
        parts.append(jnp.dot(weight, vals[:, cols], preferred_element_type=jnp.float32))
    return (jnp.stack(peaks, axis=1), jnp.stack(totals, axis=1), jnp.concatenate(parts, axis=1))

def combine(first, second):
    head_size = D // H
    peak = jnp.maximum(first[0], second[0])
    fa = jnp.exp(first[0] - peak)
    fb = jnp.exp(second[0] - peak)
    total = first[1] * fa + second[1] * fb
    merged = first[2] * jnp.repeat(fa, head_size, axis=1) + second[2] * jnp.repeat(fb, head_size, axis=1)
    return (peak, total, merged)

def reference(latents, tokens, w_query, w_key, w_value, w_out):
    head_size = D // H
    query = jnp.dot(latents, w_query, preferred_element_type=jnp.float32).astype(jnp.bfloat16)
    blocks = tokens.reshape(N_TM * N_PATCH, TOK_DEV, D)
    start = block_part(query, blocks[0], w_key, w_value)

    def step(carry, block):
        return (combine(carry, block_part(query, block, w_key, w_value)), None)
    result, _ = lax.scan(step, start, blocks[1:])
    attended = result[2] / jnp.repeat(result[1], head_size, axis=1)
    normed = (attended * lax.rsqrt(lax.optimization_barrier(jnp.mean(attended * attended, axis=1, keepdims=True)) + 1e-06)).astype(jnp.bfloat16)
    return jnp.dot(normed, w_out, preferred_element_type=jnp.float32).astype(jnp.bfloat16)
```

```python
import functools
import math

import jax
import jax.numpy as jnp
from jax import lax
from jax.experimental import pallas as pl
from jax.experimental.pallas import tpu as pltpu
from jax.sharding import PartitionSpec as P

H = 8
CORES = 2
AXES = ("tm", "patch")
VMEM = pl.BlockSpec(memory_space=pltpu.VMEM)
SMEM = pl.BlockSpec(memory_space=pltpu.SMEM)
PARAMS = pltpu.CompilerParams(vmem_limit_bytes=48 * 2**20)
EXTRA = 8


def xor_permute(value, n, step):
    return lax.ppermute(value, AXES, [(i, i ^ step) for i in range(n)])


def project_kernel(a_ref, w_ref, o_ref):
    o_ref[...] = jnp.dot(a_ref[...], w_ref[...], preferred_element_type=jnp.float32).astype(o_ref.dtype)


def project_t_kernel(a_ref, w_ref, o_ref):
    o_ref[...] = jnp.dot(a_ref[...], w_ref[...], preferred_element_type=jnp.float32).astype(o_ref.dtype).T


def project(a, w, transposed, rows=256):
    n, d = a.shape
    cols = w.shape[1]
    if transposed:
        kernel, out, spec = project_t_kernel, (cols, n), pl.BlockSpec((cols, rows), lambda i: (0, i))
    else:
        kernel, out, spec = project_kernel, (n, cols), pl.BlockSpec((rows, cols), lambda i: (i, 0))
    return pl.pallas_call(
        kernel,
        grid=(n // rows,),
        out_shape=jax.ShapeDtypeStruct(out, jnp.bfloat16),
        in_specs=[pl.BlockSpec((rows, d), lambda i: (i, 0)), pl.BlockSpec((d, cols), lambda i: (0, 0))],
        out_specs=spec,
        compiler_params=PARAMS,
        cost_estimate=pl.CostEstimate(flops=2 * n * d * cols, bytes_accessed=2 * (n * d + d * cols + n * cols), transcendentals=0),
    )(a, w)


def attend_kernel(tile, chunk, head_ref, q_ref, k_ref, v_ref, o_ref, s0, s1):
    size, latents = q_ref.shape
    tokens = k_ref.shape[0]
    n_x, n_tm, rows, block = o_ref.shape
    feats = rows - EXTRA
    coef = math.log2(math.e) / math.sqrt(size)
    slots = (s0, s1)
    ones = jnp.ones((16, chunk), jnp.bfloat16)
    row = lax.broadcasted_iota(jnp.int32, (EXTRA, tile), 0)
    peak = None
    for j in range(latents // tile + 1):
        scores, weights = j < latents // tile, j > 0
        now, before = slots[j % 2], slots[(j - 1) % 2]
        acc, top = jnp.zeros((size + 16, tile), jnp.float32), None
        for c in range(tokens // chunk):
            part = slice(c * chunk, (c + 1) * chunk)
            if scores:
                s = jnp.dot(k_ref[part, :], q_ref[:, j * tile : (j + 1) * tile], preferred_element_type=jnp.float32)
                now[part, :] = s
                high = jnp.max(s.reshape(chunk // 8, 8, tile), axis=0)
                top = high if top is None else jnp.maximum(top, high)
            if weights:
                w = jnp.exp2((before[part, :] - peak) * coef).astype(jnp.bfloat16)
                v = jnp.concatenate([v_ref[:, part], ones], axis=0)
                acc = acc + jnp.dot(v, w, preferred_element_type=jnp.float32)
        if weights:
            tail = jnp.where(row == 1, peak * coef, acc[size : size + EXTRA])
            for b in range(tile // block):
                lanes = slice(b * block, (b + 1) * block)
                tm = (j - 1) * (tile // block) + b
                for x in range(n_x):
                    o_ref[x, tm, :feats] = acc[x * feats : (x + 1) * feats, lanes]
                    o_ref[x, tm, feats:] = tail[:, lanes]
        if scores:
            peak = jnp.max(top, axis=0, keepdims=True)


def attend(head, query_t, keys, vals_t, n_x, n_tm, tile=512, chunk=1024):
    size, latents, tokens = query_t.shape[0] // H, query_t.shape[1], keys.shape[0]
    shape = (n_x, n_tm, size // n_x + EXTRA, latents // n_tm)
    return pl.pallas_call(
        functools.partial(attend_kernel, tile, chunk),
        grid_spec=pltpu.PrefetchScalarGridSpec(
            num_scalar_prefetch=1,
            grid=(1,),
            in_specs=[
                pl.BlockSpec((size, latents), lambda i, h: (h[0], 0)),
                pl.BlockSpec((tokens, size), lambda i, h: (0, h[0])),
                pl.BlockSpec((size, tokens), lambda i, h: (h[0], 0)),
            ],
            out_specs=pl.BlockSpec(shape, lambda i, h: (0, 0, 0, 0)),
            scratch_shapes=[pltpu.VMEM((tokens, tile), jnp.float32)] * 2,
        ),
        out_shape=jax.ShapeDtypeStruct(shape, jnp.float32),
        compiler_params=PARAMS,
        cost_estimate=pl.CostEstimate(
            flops=4 * tokens * latents * size, bytes_accessed=4 * math.prod(shape), transcendentals=tokens * latents
        ),
    )(head, query_t, keys, vals_t)


def merge(parts):
    feats = parts[0].shape[-2] - EXTRA
    peaks = [p[..., feats + 1 : feats + 2, :] for p in parts]
    peak = functools.reduce(jnp.maximum, peaks)
    total = sum(p * jnp.exp2(m - peak) for p, m in zip(parts, peaks))
    row = lax.broadcasted_iota(jnp.int32, total.shape, total.ndim - 2)
    return jnp.where(row == feats + 1, peak, total)


def merge_core_kernel(at_ref, own_ref, got_ref, *out_refs):
    x = at_ref[0]
    n_tm = own_ref.shape[1]
    for s, out in enumerate(out_refs):
        for t in range(n_tm):
            out[t] = merge([own_ref[x ^ s, t], got_ref[x ^ s, t]])


def merge_core(at, own, got):
    n_x = own.shape[0]
    return pl.pallas_call(
        merge_core_kernel,
        out_shape=[jax.ShapeDtypeStruct(own.shape[1:], jnp.float32)] * n_x,
        in_specs=[SMEM, VMEM, VMEM],
        out_specs=[VMEM] * n_x,
        compiler_params=PARAMS,
        cost_estimate=pl.CostEstimate(flops=own.size * 4, bytes_accessed=own.size * 12, transcendentals=0),
    )(at, own, got)


def merge_x_kernel(at_ref, *refs):
    n_tm = refs[0].shape[0]
    parts, outs = refs[:-n_tm], refs[-n_tm:]
    tm = at_ref[1]
    for s, out in enumerate(outs):
        out[...] = merge([p[tm ^ s] for p in parts])


def merge_x(at, parts):
    n_tm = parts[0].shape[0]
    return pl.pallas_call(
        merge_x_kernel,
        out_shape=[jax.ShapeDtypeStruct(parts[0].shape[1:], jnp.float32)] * n_tm,
        in_specs=[SMEM] + [VMEM] * len(parts),
        out_specs=[VMEM] * n_tm,
        compiler_params=PARAMS,
        cost_estimate=pl.CostEstimate(flops=parts[0].size * 8, bytes_accessed=parts[0].size * 12, transcendentals=0),
    )(at, *parts)


def attended_kernel(*refs):
    merged = merge([r[...] for r in refs[:-1]])
    feats = merged.shape[0] - EXTRA
    refs[-1][...] = merged[:feats] / merged[feats : feats + 1]


def attended(parts):
    rows, block = parts[0].shape
    return pl.pallas_call(
        attended_kernel,
        out_shape=jax.ShapeDtypeStruct((rows - EXTRA, block), jnp.float32),
        in_specs=[VMEM] * len(parts),
        out_specs=VMEM,
        compiler_params=PARAMS,
        cost_estimate=pl.CostEstimate(flops=rows * block * 32, bytes_accessed=rows * block * 36, transcendentals=0),
    )(*parts)


def finish_kernel(n_patch, at_ref, *refs):
    pieces, (w_ref, o_ref, normed) = refs[:-3], refs[-3:]
    feats = pieces[0].shape[0]
    width = feats * len(pieces)
    me = at_ref[2]
    squares = functools.reduce(lambda a, b: a + b, [jnp.square(p[...]) for p in pieces])
    scale = lax.rsqrt(jnp.sum(squares, axis=0, keepdims=True) * (1.0 / width) + 1e-06)
    for i, piece in enumerate(pieces):
        pair, owner = i // n_patch, me ^ (i % n_patch)
        head = CORES * pair + owner % CORES
        at = pl.multiple_of(head * (width // H) + owner // CORES * feats, feats)
        normed[pl.ds(at, feats), :] = (piece[...] * scale).astype(jnp.bfloat16)
    o_ref[...] = lax.dot_general(
        normed[...], w_ref[...], (((0,), (0,)), ((), ())), preferred_element_type=jnp.float32
    ).astype(jnp.bfloat16)


def finish(at, pieces, w_out, n_patch):
    block = pieces[0].shape[1]
    return pl.pallas_call(
        functools.partial(finish_kernel, n_patch),
        out_shape=jax.ShapeDtypeStruct((block, w_out.shape[1]), jnp.bfloat16),
        in_specs=[SMEM] + [VMEM] * (len(pieces) + 1),
        out_specs=VMEM,
        scratch_shapes=[pltpu.VMEM((w_out.shape[0], block), jnp.bfloat16)],
        compiler_params=PARAMS,
        cost_estimate=pl.CostEstimate(flops=2 * block * w_out.size, bytes_accessed=2 * w_out.size, transcendentals=0),
    )(at, *pieces, w_out)


def per_device(n_tm, n_patch, latents, tokens, w_query, w_key, w_value, w_out):
    n, n_x = n_tm * n_patch, n_patch // CORES
    tm, patch = lax.axis_index("tm"), lax.axis_index("patch")
    x, core = patch // CORES, patch % CORES
    at = jnp.stack([x, tm, patch]).astype(jnp.int32)

    query_t = project(latents, w_query, True)
    keys = project(tokens, w_key, False)
    vals_t = project(tokens, w_value, True)

    pieces = []
    for pair in range(H // CORES):
        other, own = (
            attend((CORES * pair + c).astype(jnp.int32).reshape(1), query_t, keys, vals_t, n_x, n_tm)
            for c in (1 - core, core)
        )
        kept, *sent = merge_core(at, own, xor_permute(other, n, 1))
        got = [xor_permute(v, n, CORES * (s + 1)) for s, v in enumerate(sent)]
        kept, *sent = merge_x(at, [kept, *got])
        got = [xor_permute(v, n, n_patch * (s + 1)) for s, v in enumerate(sent)]
        piece = attended([kept, *got])
        pieces += [piece] + [xor_permute(piece, n, s) for s in range(1, n_patch)]
    return finish(at, pieces, w_out, n_patch)


def solution(mesh):
    return jax.shard_map(
        functools.partial(per_device, mesh.shape["tm"], mesh.shape["patch"]),
        mesh=mesh,
        in_specs=(P(), P(("tm", "patch"), None), P(), P(), P(), P(None, "patch")),
        out_specs=P("tm", "patch"),
        check_vma=False,
    )
```

```python
import functools
import math

import jax
import jax.numpy as jnp
from jax import lax
from jax.experimental import pallas as pl
from jax.experimental.pallas import tpu as pltpu
from jax.sharding import PartitionSpec as P

H = 8
CORES = 2
AXES = ("tm", "patch")
VMEM = pl.BlockSpec(memory_space=pltpu.VMEM)
SMEM = pl.BlockSpec(memory_space=pltpu.SMEM)
PARAMS = pltpu.CompilerParams(vmem_limit_bytes=48 * 2**20)
EXTRA = 8
LEVELS = 30.0 * 2.0**10
UNITS = (2.0**20, 2.0**10, 1.0, 2.0**-10, 2.0**-20)


def xor_permute(value, n, step):
    return lax.ppermute(value, AXES, [(i, i ^ step) for i in range(n)])


def project_kernel(with_query, at_ref, t_ref, wk_ref, wv_ref, *refs):
    def dot(a, w):
        return jnp.dot(a[...], w[...], preferred_element_type=jnp.float32).astype(jnp.bfloat16)

    if with_query:
        l_ref, wq_ref, k_ref, v_ref, q_ref = refs
        q_ref[...] = dot(l_ref, wq_ref).T
    else:
        k_ref, v_ref = refs
    k_ref[...] = dot(t_ref, wk_ref)
    v_ref[...] = dot(t_ref, wv_ref).T


def project(at, tokens, w_key, w_value, latents=None, w_query=None, steps=4):
    (n, d), cols = tokens.shape, w_key.shape[1] // CORES
    weight = pl.BlockSpec((d, cols), lambda i, at: (0, at[3]))
    args = [tokens, w_key, w_value]
    in_specs = [pl.BlockSpec((n // steps, d), lambda i, at: (i, 0)), weight, weight]
    outs = [(n, cols), (cols, n)]
    out_specs = [
        pl.BlockSpec((n // steps, cols), lambda i, at: (i, 0)),
        pl.BlockSpec((cols, n // steps), lambda i, at: (0, i)),
    ]
    flops = 4 * n * d * cols
    if latents is not None:
        m = latents.shape[0]
        args += [latents, w_query]
        in_specs += [pl.BlockSpec((m // steps, d), lambda i, at: (i, 0)), weight]
        outs.append((cols, m))
        out_specs.append(pl.BlockSpec((cols, m // steps), lambda i, at: (0, i)))
        flops += 2 * m * d * cols
    return pl.pallas_call(
        functools.partial(project_kernel, latents is not None),
        grid_spec=pltpu.PrefetchScalarGridSpec(
            num_scalar_prefetch=1, grid=(steps,), in_specs=in_specs, out_specs=out_specs
        ),
        out_shape=[jax.ShapeDtypeStruct(s, jnp.bfloat16) for s in outs],
        compiler_params=PARAMS,
        cost_estimate=pl.CostEstimate(flops=flops, bytes_accessed=2 * (n * d + 2 * d * cols + 2 * n * cols), transcendentals=0),
    )(at, *args)


def merge(parts):
    peak = functools.reduce(jnp.maximum, [p for _, _, p in parts])
    factors = [jnp.exp2(p - peak) for _, _, p in parts]
    num, den = (
        functools.reduce(lambda a, b: a + b, [part[i] * f for part, f in zip(parts, factors)]) for i in range(2)
    )
    return num, den, peak


def nearest(value):
    return jnp.floor(value + 0.5)


def spread(value):
    place = nearest(jnp.abs(value) * LEVELS) * 2.0**-10
    power = jnp.floor(place)
    return jnp.where(value < 0, -1.0, 1.0) * (1.0 + place - power) * jnp.exp2(power - 14.0)


def gather_up(value):
    size = jnp.abs(value)
    power = jnp.clip(jnp.floor(jnp.log2(size)), -14.0, 15.0)
    return jnp.where(value < 0, -1.0, 1.0) * (power + 13.0 + size * jnp.exp2(-power)) * (2.0**10 / LEVELS)


def encode(part):
    num, den, peak = part
    mean = num / den
    most = jnp.max(jnp.abs(mean), axis=0, keepdims=True)
    exponent = jnp.ceil(jnp.log2(jnp.clip(most, 2.0**-100, 2.0**100)) + 2.0**-10)
    rest, digits = peak + jnp.log2(den), [exponent]
    for unit in UNITS[:-1]:
        digits.append(nearest(rest * (1.0 / unit)))
        rest = rest - digits[-1] * unit
    digits.append(rest * (1.0 / UNITS[-1]))
    row = lax.broadcasted_iota(jnp.int32, (EXTRA, mean.shape[1]), 0)
    tail = jnp.zeros((EXTRA, mean.shape[1]), jnp.float32)
    for i, digit in enumerate(digits):
        tail = jnp.where(row == i, digit, tail)
    return jnp.concatenate([spread(mean * jnp.exp2(-exponent)), tail], axis=0)


def decode(rows):
    feats = rows.shape[0] - EXTRA
    exponent, *digits = (rows[feats + i : feats + i + 1] for i in range(len(UNITS) + 1))
    peak = functools.reduce(lambda a, b: a + b, [d * u for d, u in zip(reversed(digits), reversed(UNITS))])
    return gather_up(rows[:feats]) * jnp.exp2(exponent), jnp.ones_like(peak), peak


def attend_kernel(tile, chunk, blocks, head_ref, q_ref, *refs):
    kv, got, (o_ref, s0, s1) = refs[: 2 * blocks], refs[2 * blocks : -3], refs[-3:]
    size, latents = q_ref.shape
    tokens = kv[0].shape[0]
    n_tm, rows, block = o_ref.shape
    coef = math.log2(math.e) / math.sqrt(size)
    slots = (s0, s1)
    ones = jnp.ones((16, chunk), jnp.bfloat16)
    items = [(j, b) for j in range(latents // tile) for b in range(blocks)]
    peak, done = None, []
    for i in range(len(items) + 1):
        now, before = slots[i % 2], slots[(i - 1) % 2]
        acc, top = jnp.zeros((size + 16, tile), jnp.float32), None
        for c in range(tokens // chunk):
            part = slice(c * chunk, (c + 1) * chunk)
            if i < len(items):
                j, b = items[i]
                s = jnp.dot(kv[2 * b][part, :], q_ref[:, j * tile : (j + 1) * tile], preferred_element_type=jnp.float32)
                now[part, :] = s
                high = jnp.max(s.reshape(chunk // 8, 8, tile), axis=0)
                top = high if top is None else jnp.maximum(top, high)
            if i > 0:
                w = jnp.exp2((before[part, :] - peak) * coef).astype(jnp.bfloat16)
                v = jnp.concatenate([kv[2 * items[i - 1][1] + 1][:, part], ones], axis=0)
                acc = acc + jnp.dot(v, w, preferred_element_type=jnp.float32)
        if i > 0:
            done.append((acc[:size], acc[size : size + 1], peak * coef))
            if len(done) == blocks:
                for b in range(tile // block):
                    tm = items[i - 1][0] * (tile // block) + b
                    lanes = slice(b * block, (b + 1) * block)
                    o_ref[tm] = encode(merge([tuple(v[:, lanes] for v in d) for d in done] + [decode(g[tm]) for g in got]))
                done = []
        if i < len(items):
            peak = jnp.max(top, axis=0, keepdims=True)


def attend(head, query_t, blocks, got, n_tm, heads, tile=512, chunk=1024):
    size, latents, tokens = query_t.shape[0] // heads, query_t.shape[1], blocks[0][0].shape[0]
    shape = (n_tm, size + EXTRA, latents // n_tm)
    whole = pl.BlockSpec(shape, lambda i, h: (0, 0, 0))
    return pl.pallas_call(
        functools.partial(attend_kernel, tile, chunk, len(blocks)),
        grid_spec=pltpu.PrefetchScalarGridSpec(
            num_scalar_prefetch=1,
            grid=(1,),
            in_specs=[pl.BlockSpec((size, latents), lambda i, h: (h[0], 0))]
            + [
                pl.BlockSpec((tokens, size), lambda i, h: (0, h[0])),
                pl.BlockSpec((size, tokens), lambda i, h: (h[0], 0)),
            ]
            * len(blocks)
            + [whole] * len(got),
            out_specs=whole,
            scratch_shapes=[pltpu.VMEM((tokens, tile), jnp.float32)] * 2,
        ),
        out_shape=jax.ShapeDtypeStruct(shape, jnp.float32),
        compiler_params=PARAMS,
        cost_estimate=pl.CostEstimate(
            flops=4 * tokens * latents * size * len(blocks),
            bytes_accessed=4 * math.prod(shape),
            transcendentals=tokens * latents * len(blocks),
        ),
    )(head.astype(jnp.int32).reshape(1), query_t, *[a for pair in blocks for a in pair], *got)


def attended_kernel(part_ref, out):
    n_tm, heads, rows, _ = part_ref.shape
    feats = rows - EXTRA
    for i in range(heads):
        num, den, _ = merge([decode(part_ref[t, i]) for t in range(n_tm)])
        out[i * feats : (i + 1) * feats, :] = num / den


def attended(parts):
    n_tm, heads, rows, block = parts.shape
    return pl.pallas_call(
        attended_kernel,
        out_shape=jax.ShapeDtypeStruct(((rows - EXTRA) * heads, block), jnp.float32),
        in_specs=[VMEM],
        out_specs=VMEM,
        compiler_params=PARAMS,
        cost_estimate=pl.CostEstimate(flops=parts.size * 4, bytes_accessed=parts.size * 4, transcendentals=0),
    )(parts)


def finish_kernel(at_ref, *refs):
    pieces, (w_ref, o_ref, normed) = refs[:-3], refs[-3:]
    feats, me = pieces[0].shape[0], at_ref[2]
    width = feats * len(pieces)
    squares = functools.reduce(lambda a, b: a + b, [jnp.square(p[...]) for p in pieces])
    scale = lax.rsqrt(jnp.sum(squares, axis=0, keepdims=True) * (1.0 / width) + 1e-06)
    for s, piece in enumerate(pieces):
        owner = me ^ s
        at = owner % CORES * (width // CORES) + owner // CORES * feats
        normed[pl.ds(pl.multiple_of(at, feats), feats), :] = (piece[...] * scale).astype(jnp.bfloat16)
    o_ref[...] = lax.dot_general(
        normed[...], w_ref[...], (((0,), (0,)), ((), ())), preferred_element_type=jnp.float32
    ).astype(jnp.bfloat16)


def finish(at, pieces, w_out):
    block = pieces[0].shape[1]
    return pl.pallas_call(
        finish_kernel,
        out_shape=jax.ShapeDtypeStruct((block, w_out.shape[1]), jnp.bfloat16),
        in_specs=[SMEM] + [VMEM] * (len(pieces) + 1),
        out_specs=VMEM,
        scratch_shapes=[pltpu.VMEM((w_out.shape[0], block), jnp.bfloat16)],
        compiler_params=PARAMS,
        cost_estimate=pl.CostEstimate(flops=2 * block * w_out.size, bytes_accessed=2 * w_out.size, transcendentals=0),
    )(at, *pieces, w_out)


def per_device(n_tm, n_patch, latents, tokens, w_query, w_key, w_value, w_out):
    n, n_x = n_tm * n_patch, n_patch // CORES
    tm, patch = lax.axis_index("tm"), lax.axis_index("patch")
    x, core = patch // CORES, patch % CORES
    at = jnp.stack([x, tm, patch, core]).astype(jnp.int32)
    heads = H // CORES
    own_heads = heads // n_x

    sibling = xor_permute(tokens, n, 1)
    keys, vals_t, query_t = project(at, tokens, w_key, w_value, latents, w_query)
    near = [(keys, vals_t)]
    both = None
    got = [[] for _ in range(own_heads)]
    mine = []
    for s in range(n_x - 1, -1, -1):
        for j in range(own_heads):
            head = (x ^ s) * own_heads + j
            if both is None:
                first = attend(head, query_t, near, [], n_tm, heads)
                sibling, first = lax.optimization_barrier((sibling, first))
                far = [tuple(project(at, sibling, w_key, w_value))]
                both = near + far
                part = attend(head, query_t, far, [first], n_tm, heads)
            else:
                part = attend(head, query_t, both, [] if s else got[j], n_tm, heads)
            query_t, part = lax.optimization_barrier((query_t, part))
            if s:
                got[j].append(xor_permute(part.astype(jnp.float16), n, CORES * s).astype(jnp.float32))
            else:
                mine.append(part.astype(jnp.float16))
    mine = lax.all_to_all(jnp.stack(mine, axis=1), "tm", 0, 0, tiled=True).astype(jnp.float32)
    pieces = [attended(mine)]
    pieces += [xor_permute(pieces[0], n, CORES * s) for s in range(1, n_x)]
    pieces = [p for piece in pieces for p in (piece, xor_permute(piece, n, 1))]
    return finish(at, pieces, w_out)


def solution(mesh):
    return jax.shard_map(
        functools.partial(per_device, mesh.shape["tm"], mesh.shape["patch"]),
        mesh=mesh,
        in_specs=(P(), P(("tm", "patch"), None), P(), P(), P(), P(None, "patch")),
        out_specs=P("tm", "patch"),
        check_vma=False,
    )
```

```python
import functools
import math

import jax
import jax.numpy as jnp
from jax import lax
from jax.experimental import pallas as pl
from jax.experimental.pallas import tpu as pltpu
from jax.sharding import PartitionSpec as P

H = 8
CORES = 2
NEAR = 2
AXES = ("tm", "patch")
VMEM = pl.BlockSpec(memory_space=pltpu.VMEM)
HBM = pl.BlockSpec(memory_space=pltpu.HBM)
SMEM = pl.BlockSpec(memory_space=pltpu.SMEM)
PARAMS = pltpu.CompilerParams(vmem_limit_bytes=24 * 2**20)
EXTRA = 8
LEVELS = 30.0 * 2.0**10
UNITS = (2.0**20, 2.0**10, 1.0, 2.0**-10, 2.0**-20)


def xor_permute(value, n, step):
    return lax.ppermute(value, AXES, [(i, i ^ step) for i in range(n)])


def dot(a, w):
    return jnp.dot(a, w, preferred_element_type=jnp.float32).astype(jnp.bfloat16)


def project_own_kernel(at_ref, t_hbm, l_hbm, wq_hbm, wk_hbm, wv_hbm, k_ref, v_ref, q_ref, wk_ref, wv_ref, wq_ref, t_ref, l_ref, sems):
    near, core = at_ref[1], at_ref[3]
    chunks, rows, _ = t_ref.shape
    cols = k_ref.shape[1]
    half = l_ref.shape[1] * l_ref.shape[2]
    columns = pl.ds(pl.multiple_of(core * cols, cols), cols)
    moves = [(wk_hbm.at[:, columns], wk_ref), (t_hbm.at[0], t_ref.at[0]), (wv_hbm.at[:, columns], wv_ref)]
    moves += [(t_hbm.at[c], t_ref.at[c]) for c in range(1, chunks)]
    moves += [(wq_hbm.at[:, columns], wq_ref), (l_hbm.at[:, near ^ 1], l_ref.at[0]), (l_hbm.at[:, near], l_ref.at[1])]
    copies = [pltpu.make_async_copy(src, dst, sems.at[i]) for i, (src, dst) in enumerate(moves)]
    for copy in copies:
        copy.start()
    for c in range(chunks):
        part = slice(c * rows, (c + 1) * rows)
        for copy in copies[:2] if c == 0 else [copies[c + 2]]:
            copy.wait()
        k_ref[part, :] = dot(t_ref[c], wk_ref[...])
        if c == 0:
            copies[2].wait()
        v_ref[:, part] = dot(t_ref[c], wv_ref[...]).T
    copies[chunks + 2].wait()
    for h in range(NEAR):
        copies[chunks + 3 + h].wait()
        q_ref[:, h * half : (h + 1) * half] = dot(l_ref[h].reshape(half, -1), wq_ref[...]).T


def project_own(at, tokens, latents, w_query, w_key, w_value, chunks=4):
    (n, d), cols = tokens.shape, w_key.shape[1] // CORES
    n_far, _, block, _ = latents.shape
    m = n_far * NEAR * block
    return pl.pallas_call(
        project_own_kernel,
        out_shape=[jax.ShapeDtypeStruct(s, jnp.bfloat16) for s in ((n, cols), (cols, n), (cols, m), (d, cols), (d, cols))],
        in_specs=[SMEM] + [HBM] * 5,
        out_specs=[VMEM] * 5,
        scratch_shapes=[
            pltpu.VMEM((d, cols), jnp.bfloat16),
            pltpu.VMEM((chunks, n // chunks, d), jnp.bfloat16),
            pltpu.VMEM((NEAR, n_far, block, d), jnp.bfloat16),
            pltpu.SemaphoreType.DMA((chunks + 5,)),
        ],
        compiler_params=pltpu.CompilerParams(vmem_limit_bytes=46 * 2**20),
        cost_estimate=pl.CostEstimate(
            flops=(4 * n + 2 * m) * d * cols, bytes_accessed=2 * (n * d + m * d + 3 * d * cols), transcendentals=0
        ),
    )(at, tokens.reshape(chunks, n // chunks, d), latents, w_query, w_key, w_value)


def project_kernel(chunks, t_ref, wk_ref, wv_ref, k_ref, v_ref):
    rows = t_ref.shape[0] // chunks
    for c in range(chunks):
        part = slice(c * rows, (c + 1) * rows)
        k_ref[part, :] = dot(t_ref[part, :], wk_ref[...])
        v_ref[:, part] = dot(t_ref[part, :], wv_ref[...]).T


def project(tokens, w_key, w_value, chunks=4):
    (n, d), cols = tokens.shape, w_key.shape[1]
    return pl.pallas_call(
        functools.partial(project_kernel, chunks),
        out_shape=[jax.ShapeDtypeStruct(s, jnp.bfloat16) for s in ((n, cols), (cols, n))],
        in_specs=[VMEM] * 3,
        out_specs=[VMEM] * 2,
        compiler_params=PARAMS,
        cost_estimate=pl.CostEstimate(flops=4 * n * d * cols, bytes_accessed=2 * (n * d + 2 * d * cols), transcendentals=0),
    )(tokens, w_key, w_value)


def merge(parts):
    peak = functools.reduce(jnp.maximum, [p for _, _, p in parts])
    factors = [jnp.exp2(p - peak) for _, _, p in parts]
    num, den = (
        functools.reduce(lambda a, b: a + b, [part[i] * f for part, f in zip(parts, factors)]) for i in range(2)
    )
    return num, den, peak


def nearest(value):
    return jnp.floor(value + 0.5)


def spread(value):
    place = nearest(jnp.abs(value) * LEVELS) * 2.0**-10
    power = jnp.floor(place)
    return jnp.where(value < 0, -1.0, 1.0) * (1.0 + place - power) * jnp.exp2(power - 14.0)


def gather_up(value):
    size = jnp.abs(value)
    power = jnp.clip(jnp.floor(jnp.log2(size)), -14.0, 15.0)
    return jnp.where(value < 0, -1.0, 1.0) * (power + 13.0 + size * jnp.exp2(-power)) * (2.0**10 / LEVELS)


def encode(part):
    num, den, peak = part
    mean = num / den
    most = jnp.max(jnp.abs(mean), axis=0, keepdims=True)
    exponent = jnp.ceil(jnp.log2(jnp.clip(most, 2.0**-100, 2.0**100)) + 2.0**-10)
    rest, digits = peak + jnp.log2(den), [exponent]
    for unit in UNITS[:-1]:
        digits.append(nearest(rest * (1.0 / unit)))
        rest = rest - digits[-1] * unit
    digits.append(rest * (1.0 / UNITS[-1]))
    row = lax.broadcasted_iota(jnp.int32, (EXTRA, mean.shape[1]), 0)
    tail = jnp.zeros((EXTRA, mean.shape[1]), jnp.float32)
    for i, digit in enumerate(digits):
        tail = jnp.where(row == i, digit, tail)
    return jnp.concatenate([spread(mean * jnp.exp2(-exponent)), tail], axis=0)


def decode(rows):
    feats = rows.shape[0] - EXTRA
    exponent, *digits = (rows[feats + i : feats + i + 1] for i in range(len(UNITS) + 1))
    peak = functools.reduce(lambda a, b: a + b, [d * u for d, u in zip(reversed(digits), reversed(UNITS))])
    return gather_up(rows[:feats]) * jnp.exp2(exponent), jnp.ones_like(peak), peak


def unpack(rows):
    feats = rows.shape[0] - EXTRA
    return rows[:feats], rows[feats : feats + 1], rows[feats + 1 : feats + 2]


def attend_kernel(chunk, half, blocks, encoded, at_ref, q_ref, *refs):
    kv, got, (o_ref, s0, s1) = refs[: 2 * blocks], refs[2 * blocks : -3], refs[-3:]
    tokens, lanes = s0.shape
    heads, n_far, rows, block = o_ref.shape
    size = rows - EXTRA
    coef = math.log2(math.e) / math.sqrt(size)
    slots = (s0, s1)
    ones = jnp.ones((16, chunk), jnp.bfloat16)
    row = lax.broadcasted_iota(jnp.int32, (EXTRA, lanes), 0)
    items = [(j, b) for j in range(heads) for b in range(blocks)]

    def columns(j):
        return pl.ds(pl.multiple_of((at_ref[0] * heads + j) * size, size), size)

    peak, done = None, []
    for i in range(len(items) + 1):
        now, before = slots[i % 2], slots[(i - 1) % 2]
        acc, top = jnp.zeros((size + 16, lanes), jnp.float32), None
        for c in range(tokens // chunk):
            part = slice(c * chunk, (c + 1) * chunk)
            if i < len(items):
                j, b = items[i]
                q = q_ref[columns(j), half * lanes : (half + 1) * lanes]
                s = jnp.dot(kv[2 * b][part, columns(j)], q, preferred_element_type=jnp.float32)
                now[part, :] = s
                high = jnp.max(s.reshape(chunk // 8, 8, lanes), axis=0)
                top = high if top is None else jnp.maximum(top, high)
            if i > 0:
                j, b = items[i - 1]
                w = jnp.exp2((before[part, :] - peak) * coef).astype(jnp.bfloat16)
                v = jnp.concatenate([kv[2 * b + 1][columns(j), part], ones], axis=0)
                acc = acc + jnp.dot(v, w, preferred_element_type=jnp.float32)
        if i > 0:
            j = items[i - 1][0]
            done.append((acc[:size], acc[size : size + 1], peak * coef))
            if len(done) == blocks:
                for f in range(n_far):
                    at = slice(f * block, (f + 1) * block)
                    part = merge([tuple(v[:, at] for v in d) for d in done] + [unpack(g[j, f]) for g in got])
                    if encoded:
                        o_ref[j, f] = encode(part)
                    else:
                        num, den, high = part
                        o_ref[j, f, :size] = num
                        o_ref[j, f, size:] = jnp.where(row[:, at] == 0, den, high)
                done = []
        if i < len(items):
            peak = jnp.max(top, axis=0, keepdims=True)


def attend(group, half, query_t, blocks, got, shape, encoded, chunk=1024):
    heads, n_far, rows, block = shape
    lanes, tokens = n_far * block, blocks[0][0].shape[0]
    return pl.pallas_call(
        functools.partial(attend_kernel, chunk, half, len(blocks), encoded),
        out_shape=jax.ShapeDtypeStruct(shape, jnp.float32),
        in_specs=[SMEM] + [VMEM] * (1 + 2 * len(blocks) + len(got)),
        out_specs=VMEM,
        scratch_shapes=[pltpu.VMEM((tokens, lanes), jnp.float32)] * 2,
        compiler_params=PARAMS,
        cost_estimate=pl.CostEstimate(
            flops=4 * tokens * lanes * (rows - EXTRA) * heads * len(blocks),
            bytes_accessed=4 * math.prod(shape),
            transcendentals=tokens * lanes * heads * len(blocks),
        ),
    )(group.astype(jnp.int32).reshape(1), query_t, *[a for pair in blocks for a in pair], *got)


def combine_kernel(far_first, own_ref, *refs):
    got, out = refs[:-1], refs[-1]
    heads, n_far = own_ref.shape[:2]
    for j in range(heads):
        for f in range(n_far):
            part = encode(merge([unpack(own_ref[j, f])] + [decode(g[j, f]) for g in got]))
            if far_first:
                out[f, j] = part
            else:
                out[j, f] = part


def combine(own, got, far_first):
    heads, n_far, rows, block = own.shape
    shape = (n_far, heads, rows, block) if far_first else own.shape
    return pl.pallas_call(
        functools.partial(combine_kernel, far_first),
        out_shape=jax.ShapeDtypeStruct(shape, jnp.float32),
        in_specs=[VMEM] * (1 + len(got)),
        out_specs=VMEM,
        compiler_params=PARAMS,
        cost_estimate=pl.CostEstimate(flops=own.size * 20, bytes_accessed=own.size * 12, transcendentals=0),
    )(own, *got)


def attended_kernel(part_ref, out):
    n_tm, heads, rows, _ = part_ref.shape
    feats = rows - EXTRA
    for i in range(heads):
        num, den, _ = merge([decode(part_ref[t, i]) for t in range(n_tm)])
        out[i * feats : (i + 1) * feats, :] = num / den


def attended(parts):
    n_tm, heads, rows, block = parts.shape
    return pl.pallas_call(
        attended_kernel,
        out_shape=jax.ShapeDtypeStruct(((rows - EXTRA) * heads, block), jnp.float32),
        in_specs=[VMEM],
        out_specs=VMEM,
        compiler_params=PARAMS,
        cost_estimate=pl.CostEstimate(flops=parts.size * 4, bytes_accessed=parts.size * 4, transcendentals=0),
    )(parts)


def finish_kernel(at_ref, *refs):
    pieces, (w_ref, o_ref, normed) = refs[:-3], refs[-3:]
    feats, me = pieces[0].shape[0], at_ref[2]
    width = feats * len(pieces)
    squares = functools.reduce(lambda a, b: a + b, [jnp.square(p[...]) for p in pieces])
    scale = lax.rsqrt(jnp.sum(squares, axis=0, keepdims=True) * (1.0 / width) + 1e-06)
    for s, piece in enumerate(pieces):
        owner = me ^ s
        at = owner % CORES * (width // CORES) + owner // CORES * feats
        normed[pl.ds(pl.multiple_of(at, feats), feats), :] = (piece[...] * scale).astype(jnp.bfloat16)
    o_ref[...] = lax.dot_general(
        normed[...], w_ref[...], (((0,), (0,)), ((), ())), preferred_element_type=jnp.float32
    ).astype(jnp.bfloat16)


def finish(at, pieces, w_out):
    block = pieces[0].shape[1]
    return pl.pallas_call(
        finish_kernel,
        out_shape=jax.ShapeDtypeStruct((block, w_out.shape[1]), jnp.bfloat16),
        in_specs=[SMEM] + [VMEM] * (len(pieces) + 1),
        out_specs=VMEM,
        scratch_shapes=[pltpu.VMEM((w_out.shape[0], block), jnp.bfloat16)],
        compiler_params=PARAMS,
        cost_estimate=pl.CostEstimate(flops=2 * block * w_out.size, bytes_accessed=2 * w_out.size, transcendentals=0),
    )(at, *pieces, w_out)


def narrow(part):
    return part.astype(jnp.float16)


def wide(part):
    return part.astype(jnp.float32)


def per_device(n_tm, n_patch, latents, tokens, w_query, w_key, w_value, w_out):
    n, n_x, n_far = n_tm * n_patch, n_patch // CORES, n_tm // NEAR
    tm, patch = lax.axis_index("tm"), lax.axis_index("patch")
    x, core = patch // CORES, patch % CORES
    at = jnp.stack([x, tm % NEAR, patch, core]).astype(jnp.int32)
    heads = H // n_patch
    block, d = latents.shape[0] // n_tm, latents.shape[1]
    shape = (heads, n_far, d // H + EXTRA, block)

    sibling = xor_permute(tokens, n, 1)
    latents = latents.reshape(n_far, NEAR, block, d)
    keys, vals_t, query_t, own_key, own_value = project_own(at, tokens, latents, w_query, w_key, w_value)
    near = [(keys, vals_t)]
    both = None
    got = [[], []]
    for s in range(n_x - 1, -1, -1):
        group = x ^ s
        for half in range(2):
            if both is None:
                part = attend(group, half, query_t, near, [], shape, False)
                sibling, part = lax.optimization_barrier((sibling, part))
                far = [tuple(project(sibling, own_key, own_value))]
                both = near + far
                part = attend(group, half, query_t, far, [part], shape, True)
            else:
                part = attend(group, half, query_t, both, [], shape, s > 0)
            query_t, part = lax.optimization_barrier((query_t, part))
            if s:
                got[half].append(wide(xor_permute(narrow(part), n, CORES * s)))
            elif half == 0:
                part = combine(part, got[0], False)
                got[1].append(wide(xor_permute(narrow(part), n, n_patch)))
            else:
                part = combine(part, got[1], True)
    groups = [[f * NEAR + k for f in range(n_far)] for k in range(NEAR)]
    part = wide(lax.all_to_all(narrow(part), "tm", 0, 0, axis_index_groups=groups, tiled=True))
    pieces = [attended(part)]
    pieces += [xor_permute(pieces[0], n, CORES * s) for s in range(1, n_x)]
    pieces = [p for piece in pieces for p in (piece, xor_permute(piece, n, 1))]
    return finish(at, pieces, w_out)


def solution(mesh):
    return jax.shard_map(
        functools.partial(per_device, mesh.shape["tm"], mesh.shape["patch"]),
        mesh=mesh,
        in_specs=(P(), P(("tm", "patch"), None), P(), P(), P(), P(None, "patch")),
        out_specs=P("tm", "patch"),
        check_vma=False,
    )
```

```python
import functools
import math

import jax
import jax.numpy as jnp
from jax import lax
from jax.experimental import pallas as pl
from jax.experimental.pallas import tpu as pltpu
from jax.sharding import PartitionSpec as P

H = 8
CORES = 2
NEAR = 2
AXES = ("tm", "patch")
VMEM = pl.BlockSpec(memory_space=pltpu.VMEM)
HBM = pl.BlockSpec(memory_space=pltpu.HBM)
SMEM = pl.BlockSpec(memory_space=pltpu.SMEM)
PARAMS = pltpu.CompilerParams(vmem_limit_bytes=24 * 2**20)
EXTRA = 8
LEVELS = 30.0 * 2.0**10
UNITS = (2.0**20, 2.0**10, 1.0, 2.0**-10, 2.0**-20)


def xor_permute(value, n, step):
    return lax.ppermute(value, AXES, [(i, i ^ step) for i in range(n)])


def dot(a, w):
    return jnp.dot(a, w, preferred_element_type=jnp.float32).astype(jnp.bfloat16)


def project_own_kernel(at_ref, t_hbm, l_hbm, wq_hbm, wk_hbm, wv_hbm, k_ref, v_ref, q_ref, wk_ref, wv_ref, wq_ref, t_ref, l_ref, sems):
    near, core = at_ref[1], at_ref[3]
    chunks, rows, _ = t_ref.shape
    cols = k_ref.shape[1]
    half = l_ref.shape[1] * l_ref.shape[2]
    columns = pl.ds(pl.multiple_of(core * cols, cols), cols)
    moves = [(wk_hbm.at[:, columns], wk_ref), (t_hbm.at[0], t_ref.at[0]), (wv_hbm.at[:, columns], wv_ref)]
    moves += [(t_hbm.at[c], t_ref.at[c]) for c in range(1, chunks)]
    moves += [(wq_hbm.at[:, columns], wq_ref), (l_hbm.at[:, near ^ 1], l_ref.at[0]), (l_hbm.at[:, near], l_ref.at[1])]
    copies = [pltpu.make_async_copy(src, dst, sems.at[i]) for i, (src, dst) in enumerate(moves)]
    for copy in copies[:3]:
        copy.start()
    for c in range(chunks):
        part = slice(c * rows, (c + 1) * rows)
        for copy in copies[:2] if c == 0 else [copies[c + 2]]:
            copy.wait()
        if c == 0:
            for copy in copies[3:]:
                copy.start()
        k_ref[part, :] = dot(t_ref[c], wk_ref[...])
        if c == 0:
            copies[2].wait()
        v_ref[:, part] = dot(t_ref[c], wv_ref[...]).T
    copies[chunks + 2].wait()
    for h in range(NEAR):
        copies[chunks + 3 + h].wait()
        q_ref[:, h * half : (h + 1) * half] = dot(l_ref[h].reshape(half, -1), wq_ref[...]).T


def project_own(at, tokens, latents, w_query, w_key, w_value, chunks=2):
    (n, d), cols = tokens.shape, w_key.shape[1] // CORES
    n_far, _, block, _ = latents.shape
    m = n_far * NEAR * block
    return pl.pallas_call(
        project_own_kernel,
        out_shape=[jax.ShapeDtypeStruct(s, jnp.bfloat16) for s in ((n, cols), (cols, n), (cols, m), (d, cols), (d, cols))],
        in_specs=[SMEM] + [HBM] * 5,
        out_specs=[VMEM] * 5,
        scratch_shapes=[
            pltpu.VMEM((d, cols), jnp.bfloat16),
            pltpu.VMEM((chunks, n // chunks, d), jnp.bfloat16),
            pltpu.VMEM((NEAR, n_far, block, d), jnp.bfloat16),
            pltpu.SemaphoreType.DMA((chunks + 5,)),
        ],
        compiler_params=pltpu.CompilerParams(vmem_limit_bytes=46 * 2**20),
        cost_estimate=pl.CostEstimate(
            flops=(4 * n + 2 * m) * d * cols, bytes_accessed=2 * (n * d + m * d + 3 * d * cols), transcendentals=0
        ),
    )(at, tokens.reshape(chunks, n // chunks, d), latents, w_query, w_key, w_value)


def project_kernel(chunks, t_ref, wk_ref, wv_ref, k_ref, v_ref):
    rows = t_ref.shape[0] // chunks
    for c in range(chunks):
        part = slice(c * rows, (c + 1) * rows)
        k_ref[part, :] = dot(t_ref[part, :], wk_ref[...])
        v_ref[:, part] = dot(t_ref[part, :], wv_ref[...]).T


def project(tokens, w_key, w_value, chunks=2):
    (n, d), cols = tokens.shape, w_key.shape[1]
    return pl.pallas_call(
        functools.partial(project_kernel, chunks),
        out_shape=[jax.ShapeDtypeStruct(s, jnp.bfloat16) for s in ((n, cols), (cols, n))],
        in_specs=[VMEM] * 3,
        out_specs=[VMEM] * 2,
        compiler_params=PARAMS,
        cost_estimate=pl.CostEstimate(flops=4 * n * d * cols, bytes_accessed=2 * (n * d + 2 * d * cols), transcendentals=0),
    )(tokens, w_key, w_value)


def merge(parts):
    peak = functools.reduce(jnp.maximum, [p for _, _, p in parts])
    factors = [jnp.exp2(p - peak) for _, _, p in parts]
    num, den = (
        functools.reduce(lambda a, b: a + b, [part[i] * f for part, f in zip(parts, factors)]) for i in range(2)
    )
    return num, den, peak


def nearest(value):
    return jnp.floor(value + 0.5)


def spread(value):
    place = nearest(jnp.abs(value) * LEVELS) * 2.0**-10
    power = jnp.floor(place)
    return jnp.where(value < 0, -1.0, 1.0) * (1.0 + place - power) * jnp.exp2(power - 14.0)


def gather_up(value):
    size = jnp.abs(value)
    power = jnp.clip(jnp.floor(jnp.log2(size)), -14.0, 15.0)
    return jnp.where(value < 0, -1.0, 1.0) * (power + 13.0 + size * jnp.exp2(-power)) * (2.0**10 / LEVELS)


def encode(part):
    num, den, peak = part
    mean = num / den
    most = jnp.max(jnp.abs(mean), axis=0, keepdims=True)
    exponent = jnp.ceil(jnp.log2(jnp.clip(most, 2.0**-100, 2.0**100)) + 2.0**-10)
    rest, digits = peak + jnp.log2(den), [exponent]
    for unit in UNITS[:-1]:
        digits.append(nearest(rest * (1.0 / unit)))
        rest = rest - digits[-1] * unit
    digits.append(rest * (1.0 / UNITS[-1]))
    row = lax.broadcasted_iota(jnp.int32, (EXTRA, mean.shape[1]), 0)
    tail = jnp.zeros((EXTRA, mean.shape[1]), jnp.float32)
    for i, digit in enumerate(digits):
        tail = jnp.where(row == i, digit, tail)
    return jnp.concatenate([spread(mean * jnp.exp2(-exponent)), tail], axis=0)


def decode(rows):
    feats = rows.shape[0] - EXTRA
    exponent, *digits = (rows[feats + i : feats + i + 1] for i in range(len(UNITS) + 1))
    peak = functools.reduce(lambda a, b: a + b, [d * u for d, u in zip(reversed(digits), reversed(UNITS))])
    return gather_up(rows[:feats]) * jnp.exp2(exponent), jnp.ones_like(peak), peak


def unpack(rows):
    feats = rows.shape[0] - EXTRA
    return rows[:feats], rows[feats : feats + 1], rows[feats + 1 : feats + 2]


def pack(part):
    num, den, peak = part
    row = lax.broadcasted_iota(jnp.int32, (EXTRA, num.shape[1]), 0)
    return jnp.concatenate([num, jnp.where(row == 0, den, peak)], axis=0)


def attend_kernel(chunk, half, blocks, encoded, at_ref, q_ref, *refs):
    kv, got, (o_ref, s0, s1) = refs[: 2 * blocks], refs[2 * blocks : -3], refs[-3:]
    tokens, lanes = s0.shape
    heads, n_far, rows, block = o_ref.shape
    size = rows - EXTRA
    coef = math.log2(math.e) / math.sqrt(size)
    slots = (s0, s1)
    ones = jnp.ones((16, chunk), jnp.bfloat16)
    items = [(j, b) for j in range(heads) for b in range(blocks)]

    def columns(j):
        return pl.ds(pl.multiple_of((at_ref[0] * heads + j) * size, size), size)

    peak, done = None, []
    for i in range(len(items) + 1):
        now, before = slots[i % 2], slots[(i - 1) % 2]
        acc, top = jnp.zeros((size + 16, lanes), jnp.float32), None
        for c in range(tokens // chunk):
            part = slice(c * chunk, (c + 1) * chunk)
            if i < len(items):
                j, b = items[i]
                q = q_ref[columns(j), half * lanes : (half + 1) * lanes]
                s = jnp.dot(kv[2 * b][part, columns(j)], q, preferred_element_type=jnp.float32)
                now[part, :] = s
                high = jnp.max(s.reshape(chunk // 8, 8, lanes), axis=0)
                top = high if top is None else jnp.maximum(top, high)
            if i > 0:
                j, b = items[i - 1]
                w = jnp.exp2((before[part, :] - peak) * coef).astype(jnp.bfloat16)
                v = jnp.concatenate([kv[2 * b + 1][columns(j), part], ones], axis=0)
                acc = acc + jnp.dot(v, w, preferred_element_type=jnp.float32)
        if i > 0:
            j = items[i - 1][0]
            done.append((acc[:size], acc[size : size + 1], peak * coef))
            if len(done) == blocks:
                for f in range(n_far):
                    at = slice(f * block, (f + 1) * block)
                    part = merge([tuple(v[:, at] for v in d) for d in done] + [unpack(g[j, f]) for g in got])
                    o_ref[j, f] = encode(part) if encoded else pack(part)
                done = []
        if i < len(items):
            peak = jnp.max(top, axis=0, keepdims=True)


def attend(group, half, query_t, blocks, got, shape, encoded, chunk=1024):
    heads, n_far, rows, block = shape
    lanes, tokens = n_far * block, blocks[0][0].shape[0]
    return pl.pallas_call(
        functools.partial(attend_kernel, chunk, half, len(blocks), encoded),
        out_shape=jax.ShapeDtypeStruct(shape, jnp.float32),
        in_specs=[SMEM] + [VMEM] * (1 + 2 * len(blocks) + len(got)),
        out_specs=VMEM,
        scratch_shapes=[pltpu.VMEM((tokens, lanes), jnp.float32)] * 2,
        compiler_params=PARAMS,
        cost_estimate=pl.CostEstimate(
            flops=4 * tokens * lanes * (rows - EXTRA) * heads * len(blocks),
            bytes_accessed=4 * math.prod(shape),
            transcendentals=tokens * lanes * heads * len(blocks),
        ),
    )(group.astype(jnp.int32).reshape(1), query_t, *[a for pair in blocks for a in pair], *got)


def combine_kernel(own_ref, *refs):
    got, out = refs[:-1], refs[-1]
    heads, n_far = own_ref.shape[:2]
    for j in range(heads):
        for f in range(n_far):
            out[j, f] = encode(merge([unpack(own_ref[j, f])] + [decode(g[j, f]) for g in got]))


def combine(own, got):
    return pl.pallas_call(
        combine_kernel,
        out_shape=jax.ShapeDtypeStruct(own.shape, jnp.float32),
        in_specs=[VMEM] * (1 + len(got)),
        out_specs=VMEM,
        compiler_params=PARAMS,
        cost_estimate=pl.CostEstimate(flops=own.size * 20, bytes_accessed=own.size * 12, transcendentals=0),
    )(own, *got)


def scatter_kernel(n_far, at_ref, own_ref, *refs):
    got, outs = refs[:-n_far], refs[-n_far:]
    far = at_ref[4]
    for s, out in enumerate(outs):
        for j in range(own_ref.shape[0]):
            part = merge([unpack(own_ref[j, far ^ s])] + [decode(g[j, far ^ s]) for g in got])
            out[j] = encode(part) if s else pack(part)


def scatter(at, own, got):
    heads, n_far, rows, block = own.shape
    return pl.pallas_call(
        functools.partial(scatter_kernel, n_far),
        out_shape=[jax.ShapeDtypeStruct((heads, rows, block), jnp.float32)] * n_far,
        in_specs=[SMEM] + [VMEM] * (1 + len(got)),
        out_specs=[VMEM] * n_far,
        compiler_params=PARAMS,
        cost_estimate=pl.CostEstimate(flops=own.size * 20, bytes_accessed=own.size * 12, transcendentals=0),
    )(at, own, *got)


def attended_kernel(own_ref, *refs):
    got, out = refs[:-1], refs[-1]
    heads, rows, _ = own_ref.shape
    feats = rows - EXTRA
    for i in range(heads):
        num, den, _ = merge([unpack(own_ref[i])] + [decode(g[i]) for g in got])
        out[i * feats : (i + 1) * feats, :] = num / den


def attended(own, got):
    heads, rows, block = own.shape
    return pl.pallas_call(
        attended_kernel,
        out_shape=jax.ShapeDtypeStruct(((rows - EXTRA) * heads, block), jnp.float32),
        in_specs=[VMEM] * (1 + len(got)),
        out_specs=VMEM,
        compiler_params=PARAMS,
        cost_estimate=pl.CostEstimate(flops=own.size * 20, bytes_accessed=own.size * 16, transcendentals=0),
    )(own, *got)


def finish_kernel(at_ref, *refs):
    pieces, (w_ref, o_ref, normed) = refs[:-3], refs[-3:]
    feats, me = pieces[0].shape[0], at_ref[2]
    width = feats * len(pieces)
    squares = functools.reduce(lambda a, b: a + b, [jnp.square(p[...]) for p in pieces])
    scale = lax.rsqrt(jnp.sum(squares, axis=0, keepdims=True) * (1.0 / width) + 1e-06)
    for s, piece in enumerate(pieces):
        owner = me ^ s
        at = owner % CORES * (width // CORES) + owner // CORES * feats
        normed[pl.ds(pl.multiple_of(at, feats), feats), :] = (piece[...] * scale).astype(jnp.bfloat16)
    o_ref[...] = lax.dot_general(
        normed[...], w_ref[...], (((0,), (0,)), ((), ())), preferred_element_type=jnp.float32
    ).astype(jnp.bfloat16)


def finish(at, pieces, w_out):
    block = pieces[0].shape[1]
    return pl.pallas_call(
        finish_kernel,
        out_shape=jax.ShapeDtypeStruct((block, w_out.shape[1]), jnp.bfloat16),
        in_specs=[SMEM] + [VMEM] * (len(pieces) + 1),
        out_specs=VMEM,
        scratch_shapes=[pltpu.VMEM((w_out.shape[0], block), jnp.bfloat16)],
        compiler_params=PARAMS,
        cost_estimate=pl.CostEstimate(flops=2 * block * w_out.size, bytes_accessed=2 * w_out.size, transcendentals=0),
    )(at, *pieces, w_out)


def narrow(part):
    return part.astype(jnp.float16)


def wide(part):
    return part.astype(jnp.float32)


def per_device(n_tm, n_patch, latents, tokens, w_query, w_key, w_value, w_out):
    n, n_x, n_far = n_tm * n_patch, n_patch // CORES, n_tm // NEAR
    tm, patch = lax.axis_index("tm"), lax.axis_index("patch")
    x, core = patch // CORES, patch % CORES
    at = jnp.stack([x, tm % NEAR, patch, core, tm // NEAR]).astype(jnp.int32)
    heads = H // n_patch
    block, d = latents.shape[0] // n_tm, latents.shape[1]
    shape = (heads, n_far, d // H + EXTRA, block)

    sibling = xor_permute(tokens, n, 1)
    latents = latents.reshape(n_far, NEAR, block, d)
    keys, vals_t, query_t, own_key, own_value = project_own(at, tokens, latents, w_query, w_key, w_value)
    near = [(keys, vals_t)]
    both = None
    got = [[], []]
    for s in range(n_x - 1, -1, -1):
        group = x ^ s
        for half in range(2):
            if both is None:
                part = attend(group, half, query_t, near, [], shape, False)
                sibling, part = lax.optimization_barrier((sibling, part))
                far = [tuple(project(sibling, own_key, own_value))]
                both = near + far
                part = attend(group, half, query_t, far, [part], shape, True)
            else:
                part = attend(group, half, query_t, both, [], shape, s > 0)
            query_t, part = lax.optimization_barrier((query_t, part))
            if s:
                got[half].append(wide(xor_permute(narrow(part), n, CORES * s)))
            elif half == 0:
                part = combine(part, got[0])
                got[1].append(wide(xor_permute(narrow(part), n, n_patch)))
            else:
                mine, *sent = scatter(at, part, got[1])
    far_got = {}
    for s in sorted(range(1, n_far), key=lambda s: (-s.bit_length(), s)):
        far_got[s] = wide(xor_permute(narrow(sent[s - 1]), n, n_patch * NEAR * s))
    pieces = [attended(mine, [far_got[s] for s in range(1, n_far)])]
    pieces += [xor_permute(pieces[0], n, CORES * s) for s in range(1, n_x)]
    pieces = [p for piece in pieces for p in (piece, xor_permute(piece, n, 1))]
    return finish(at, pieces, w_out)


def solution(mesh):
    return jax.shard_map(
        functools.partial(per_device, mesh.shape["tm"], mesh.shape["patch"]),
        mesh=mesh,
        in_specs=(P(), P(("tm", "patch"), None), P(), P(), P(), P(None, "patch")),
        out_specs=P("tm", "patch"),
        check_vma=False,
    )
```

```python
import functools
import math

import jax
import jax.numpy as jnp
from jax import lax
from jax.experimental import pallas as pl
from jax.experimental.pallas import tpu as pltpu
from jax.sharding import PartitionSpec as P

H = 8
CORES = 2
NEAR = 2
AXES = ("tm", "patch")
VMEM = pl.BlockSpec(memory_space=pltpu.VMEM)
HBM = pl.BlockSpec(memory_space=pltpu.HBM)
SMEM = pl.BlockSpec(memory_space=pltpu.SMEM)
PARAMS = pltpu.CompilerParams(vmem_limit_bytes=24 * 2**20)
EXTRA = 8
LEVELS = 30.0 * 2.0**10
UNITS = (2.0**20, 2.0**10, 1.0, 2.0**-10, 2.0**-20)


def xor_permute(value, n, step):
    return lax.ppermute(value, AXES, [(i, i ^ step) for i in range(n)])


def dot(a, w):
    return jnp.dot(a, w, preferred_element_type=jnp.float32).astype(jnp.bfloat16)


def project_own_kernel(at_ref, t_hbm, l_hbm, wq_hbm, wk_hbm, wv_hbm, k_ref, v_ref, q_ref, wk_ref, wv_ref, wq_ref, t_ref, l_ref, sems):
    near, core = at_ref[1], at_ref[3]
    n = t_ref.shape[0]
    cols = k_ref.shape[1]
    half = l_ref.shape[1] * l_ref.shape[2]
    columns = pl.ds(pl.multiple_of(core * cols, cols), cols)
    parts = [slice(0, n // 4), slice(n // 4, n // 2), slice(n // 2, n)]
    moves = [(wk_hbm.at[:, columns], wk_ref), (t_hbm.at[parts[0]], t_ref.at[parts[0]])]
    moves += [(wv_hbm.at[:, columns], wv_ref)] + [(t_hbm.at[p], t_ref.at[p]) for p in parts[1:]]
    moves += [(wq_hbm.at[:, columns], wq_ref), (l_hbm.at[:, near ^ 1], l_ref.at[0]), (l_hbm.at[:, near], l_ref.at[1])]
    copies = [pltpu.make_async_copy(src, dst, sems.at[i]) for i, (src, dst) in enumerate(moves)]

    def wait(*which):
        for i in which:
            copies[i].wait()

    def project_keys(part):
        k_ref[part, :] = dot(t_ref[part, :], wk_ref[...])

    def project_vals(part):
        v_ref[:, part] = dot(t_ref[part, :], wv_ref[...]).T

    for copy in copies:
        copy.start()
    wait(0, 1)
    project_keys(parts[0])
    wait(2, 3)
    project_vals(parts[0])
    project_keys(parts[1])
    project_vals(parts[1])
    wait(4)
    project_keys(parts[2])
    project_vals(parts[2])
    wait(5, 6, 7)
    for h in range(NEAR):
        q_ref[:, h * half : (h + 1) * half] = dot(l_ref[h].reshape(half, -1), wq_ref[...]).T


def project_own(at, tokens, latents, w_query, w_key, w_value):
    (n, d), cols = tokens.shape, w_key.shape[1] // CORES
    n_far, _, block, _ = latents.shape
    m = n_far * NEAR * block
    return pl.pallas_call(
        project_own_kernel,
        out_shape=[jax.ShapeDtypeStruct(s, jnp.bfloat16) for s in ((n, cols), (cols, n), (cols, m), (d, cols), (d, cols))],
        in_specs=[SMEM] + [HBM] * 5,
        out_specs=[VMEM] * 5,
        scratch_shapes=[
            pltpu.VMEM((d, cols), jnp.bfloat16),
            pltpu.VMEM((n, d), jnp.bfloat16),
            pltpu.VMEM((NEAR, n_far, block, d), jnp.bfloat16),
            pltpu.SemaphoreType.DMA((8,)),
        ],
        compiler_params=pltpu.CompilerParams(vmem_limit_bytes=46 * 2**20),
        cost_estimate=pl.CostEstimate(
            flops=(4 * n + 2 * m) * d * cols, bytes_accessed=2 * (n * d + m * d + 3 * d * cols), transcendentals=0
        ),
    )(at, tokens, latents, w_query, w_key, w_value)


def project_kernel(t_hbm, wk_ref, wv_ref, k_ref, v_ref, t_ref, sems):
    n = t_ref.shape[0]
    parts = [slice(0, n // 4), slice(n // 4, n // 2), slice(n // 2, n)]
    copies = [pltpu.make_async_copy(t_hbm.at[p], t_ref.at[p], sems.at[i]) for i, p in enumerate(parts)]
    for copy in copies:
        copy.start()
    for copy, part in zip(copies, parts):
        copy.wait()
        k_ref[part, :] = dot(t_ref[part, :], wk_ref[...])
        v_ref[:, part] = dot(t_ref[part, :], wv_ref[...]).T


def project(tokens, w_key, w_value):
    (n, d), cols = tokens.shape, w_key.shape[1]
    return pl.pallas_call(
        project_kernel,
        out_shape=[jax.ShapeDtypeStruct(s, jnp.bfloat16) for s in ((n, cols), (cols, n))],
        in_specs=[HBM, VMEM, VMEM],
        out_specs=[VMEM] * 2,
        scratch_shapes=[pltpu.VMEM((n, d), jnp.bfloat16), pltpu.SemaphoreType.DMA((3,))],
        compiler_params=PARAMS,
        cost_estimate=pl.CostEstimate(flops=4 * n * d * cols, bytes_accessed=2 * (n * d + 2 * d * cols), transcendentals=0),
    )(tokens, w_key, w_value)


def merge(parts):
    peak = functools.reduce(jnp.maximum, [p for _, _, p in parts])
    factors = [jnp.exp2(p - peak) for _, _, p in parts]
    num, den = (
        functools.reduce(lambda a, b: a + b, [part[i] * f for part, f in zip(parts, factors)]) for i in range(2)
    )
    return num, den, peak


def nearest(value):
    return jnp.floor(value + 0.5)


def spread(value):
    place = nearest(jnp.abs(value) * LEVELS) * 2.0**-10
    power = jnp.floor(place)
    return jnp.where(value < 0, -1.0, 1.0) * (1.0 + place - power) * jnp.exp2(power - 14.0)


def gather_up(value):
    size = jnp.abs(value)
    power = jnp.clip(jnp.floor(jnp.log2(size)), -14.0, 15.0)
    return jnp.where(value < 0, -1.0, 1.0) * (power + 13.0 + size * jnp.exp2(-power)) * (2.0**10 / LEVELS)


def encode(part):
    num, den, peak = part
    mean = num / den
    most = jnp.max(jnp.abs(mean), axis=0, keepdims=True)
    exponent = jnp.ceil(jnp.log2(jnp.clip(most, 2.0**-100, 2.0**100)) + 2.0**-10)
    rest, digits = peak + jnp.log2(den), [exponent]
    for unit in UNITS[:-1]:
        digits.append(nearest(rest * (1.0 / unit)))
        rest = rest - digits[-1] * unit
    digits.append(rest * (1.0 / UNITS[-1]))
    row = lax.broadcasted_iota(jnp.int32, (EXTRA, mean.shape[1]), 0)
    tail = jnp.zeros((EXTRA, mean.shape[1]), jnp.float32)
    for i, digit in enumerate(digits):
        tail = jnp.where(row == i, digit, tail)
    return jnp.concatenate([spread(mean * jnp.exp2(-exponent)), tail], axis=0)


def decode(rows):
    feats = rows.shape[0] - EXTRA
    exponent, *digits = (rows[feats + i : feats + i + 1] for i in range(len(UNITS) + 1))
    peak = functools.reduce(lambda a, b: a + b, [d * u for d, u in zip(reversed(digits), reversed(UNITS))])
    return gather_up(rows[:feats]) * jnp.exp2(exponent), jnp.ones_like(peak), peak


def unpack(rows):
    feats = rows.shape[0] - EXTRA
    return rows[:feats], rows[feats : feats + 1], rows[feats + 1 : feats + 2]


def pack(part):
    num, den, peak = part
    row = lax.broadcasted_iota(jnp.int32, (EXTRA, num.shape[1]), 0)
    return jnp.concatenate([num, jnp.where(row == 0, den, peak)], axis=0)


def attend_kernel(chunk, half, blocks, encoded, at_ref, q_ref, *refs):
    kv, got, (o_ref, s0, s1) = refs[: 2 * blocks], refs[2 * blocks : -3], refs[-3:]
    tokens, lanes = s0.shape
    heads, n_far, rows, block = o_ref.shape
    size = rows - EXTRA
    coef = math.log2(math.e) / math.sqrt(size)
    slots = (s0, s1)
    ones = jnp.ones((16, chunk), jnp.bfloat16)
    items = [(j, b) for j in range(heads) for b in range(blocks)]

    def columns(j):
        return pl.ds(pl.multiple_of((at_ref[0] * heads + j) * size, size), size)

    peak, done = None, []
    for i in range(len(items) + 1):
        now, before = slots[i % 2], slots[(i - 1) % 2]
        acc, top = jnp.zeros((size + 16, lanes), jnp.float32), None
        for c in range(tokens // chunk):
            part = slice(c * chunk, (c + 1) * chunk)
            if i < len(items):
                j, b = items[i]
                q = q_ref[columns(j), half * lanes : (half + 1) * lanes]
                s = jnp.dot(kv[2 * b][part, columns(j)], q, preferred_element_type=jnp.float32)
                now[part, :] = s
                high = jnp.max(s.reshape(chunk // 8, 8, lanes), axis=0)
                top = high if top is None else jnp.maximum(top, high)
            if i > 0:
                j, b = items[i - 1]
                w = jnp.exp2((before[part, :] - peak) * coef).astype(jnp.bfloat16)
                v = jnp.concatenate([kv[2 * b + 1][columns(j), part], ones], axis=0)
                acc = acc + jnp.dot(v, w, preferred_element_type=jnp.float32)
        if i > 0:
            j = items[i - 1][0]
            done.append((acc[:size], acc[size : size + 1], peak * coef))
            if len(done) == blocks:
                for f in range(n_far):
                    at = slice(f * block, (f + 1) * block)
                    part = merge([tuple(v[:, at] for v in d) for d in done] + [unpack(g[j, f]) for g in got])
                    o_ref[j, f] = encode(part) if encoded else pack(part)
                done = []
        if i < len(items):
            peak = jnp.max(top, axis=0, keepdims=True)


def attend(group, half, query_t, blocks, got, shape, encoded, chunk=1024):
    heads, n_far, rows, block = shape
    lanes, tokens = n_far * block, blocks[0][0].shape[0]
    return pl.pallas_call(
        functools.partial(attend_kernel, chunk, half, len(blocks), encoded),
        out_shape=jax.ShapeDtypeStruct(shape, jnp.float32),
        in_specs=[SMEM] + [VMEM] * (1 + 2 * len(blocks) + len(got)),
        out_specs=VMEM,
        scratch_shapes=[pltpu.VMEM((tokens, lanes), jnp.float32)] * 2,
        compiler_params=PARAMS,
        cost_estimate=pl.CostEstimate(
            flops=4 * tokens * lanes * (rows - EXTRA) * heads * len(blocks),
            bytes_accessed=4 * math.prod(shape),
            transcendentals=tokens * lanes * heads * len(blocks),
        ),
    )(group.astype(jnp.int32).reshape(1), query_t, *[a for pair in blocks for a in pair], *got)


def combine_kernel(encoded, own_ref, *refs):
    got, out = refs[:-1], refs[-1]
    heads, n_far = own_ref.shape[:2]
    for j in range(heads):
        for f in range(n_far):
            part = merge([unpack(own_ref[j, f])] + [decode(g[j, f]) for g in got])
            out[j, f] = encode(part) if encoded else pack(part)


def combine(own, got, encoded):
    return pl.pallas_call(
        functools.partial(combine_kernel, encoded),
        out_shape=jax.ShapeDtypeStruct(own.shape, jnp.float32),
        in_specs=[VMEM] * (1 + len(got)),
        out_specs=VMEM,
        compiler_params=PARAMS,
        cost_estimate=pl.CostEstimate(flops=own.size * 20, bytes_accessed=own.size * 12, transcendentals=0),
    )(own, *got)


def scatter_kernel(n_far, at_ref, own_ref, *refs):
    got, outs = refs[:-n_far], refs[-n_far:]
    far = at_ref[4]
    for s, out in enumerate(outs):
        for j in range(own_ref.shape[0]):
            part = merge([unpack(own_ref[j, far ^ s])] + [decode(g[j, far ^ s]) for g in got])
            out[j] = encode(part) if s else pack(part)


def scatter(at, own, got):
    heads, n_far, rows, block = own.shape
    return pl.pallas_call(
        functools.partial(scatter_kernel, n_far),
        out_shape=[jax.ShapeDtypeStruct((heads, rows, block), jnp.float32)] * n_far,
        in_specs=[SMEM] + [VMEM] * (1 + len(got)),
        out_specs=[VMEM] * n_far,
        compiler_params=PARAMS,
        cost_estimate=pl.CostEstimate(flops=own.size * 20, bytes_accessed=own.size * 12, transcendentals=0),
    )(at, own, *got)


def attended_kernel(own_ref, *refs):
    got, out = refs[:-1], refs[-1]
    heads, rows, _ = own_ref.shape
    feats = rows - EXTRA
    for i in range(heads):
        num, den, _ = merge([unpack(own_ref[i])] + [decode(g[i]) for g in got])
        out[i * feats : (i + 1) * feats, :] = num / den


def attended(own, got):
    heads, rows, block = own.shape
    return pl.pallas_call(
        attended_kernel,
        out_shape=jax.ShapeDtypeStruct(((rows - EXTRA) * heads, block), jnp.float32),
        in_specs=[VMEM] * (1 + len(got)),
        out_specs=VMEM,
        compiler_params=PARAMS,
        cost_estimate=pl.CostEstimate(flops=own.size * 20, bytes_accessed=own.size * 16, transcendentals=0),
    )(own, *got)


def finish_kernel(at_ref, *refs):
    pieces, (w_ref, o_ref, normed) = refs[:-3], refs[-3:]
    feats, me = pieces[0].shape[0], at_ref[2]
    width = feats * len(pieces)
    squares = functools.reduce(lambda a, b: a + b, [jnp.square(p[...]) for p in pieces])
    scale = lax.rsqrt(jnp.sum(squares, axis=0, keepdims=True) * (1.0 / width) + 1e-06)
    for s, piece in enumerate(pieces):
        owner = me ^ s
        at = owner % CORES * (width // CORES) + owner // CORES * feats
        normed[pl.ds(pl.multiple_of(at, feats), feats), :] = (piece[...] * scale).astype(jnp.bfloat16)
    o_ref[...] = lax.dot_general(
        normed[...], w_ref[...], (((0,), (0,)), ((), ())), preferred_element_type=jnp.float32
    ).astype(jnp.bfloat16)


def finish(at, pieces, w_out):
    block = pieces[0].shape[1]
    return pl.pallas_call(
        finish_kernel,
        out_shape=jax.ShapeDtypeStruct((block, w_out.shape[1]), jnp.bfloat16),
        in_specs=[SMEM] + [VMEM] * (len(pieces) + 1),
        out_specs=VMEM,
        scratch_shapes=[pltpu.VMEM((w_out.shape[0], block), jnp.bfloat16)],
        compiler_params=PARAMS,
        cost_estimate=pl.CostEstimate(flops=2 * block * w_out.size, bytes_accessed=2 * w_out.size, transcendentals=0),
    )(at, *pieces, w_out)


def narrow(part):
    return part.astype(jnp.float16)


def wide(part):
    return part.astype(jnp.float32)


def per_device(n_tm, n_patch, latents, tokens, w_query, w_key, w_value, w_out):
    n, n_x, n_far = n_tm * n_patch, n_patch // CORES, n_tm // NEAR
    tm, patch = lax.axis_index("tm"), lax.axis_index("patch")
    x, core = patch // CORES, patch % CORES
    at = jnp.stack([x, tm % NEAR, patch, core, tm // NEAR]).astype(jnp.int32)
    heads = H // n_patch
    block, d = latents.shape[0] // n_tm, latents.shape[1]
    shape = (heads, n_far, d // H + EXTRA, block)

    sibling = xor_permute(tokens, n, 1)
    latents = latents.reshape(n_far, NEAR, block, d)
    keys, vals_t, query_t, own_key, own_value = project_own(at, tokens, latents, w_query, w_key, w_value)
    near = [(keys, vals_t)]
    both = None
    got, across = [[], []], []
    for s in range(n_x - 1, -1, -1):
        group = x ^ s
        for half in range(2):
            if both is None:
                part = attend(group, half, query_t, near, [], shape, False)
                sibling, part = lax.optimization_barrier((sibling, part))
                far = [tuple(project(sibling, own_key, own_value))]
                both = near + far
                part = attend(group, half, query_t, far, [part], shape, True)
            else:
                part = attend(group, half, query_t, both, [], shape, s > 0)
            query_t, part = lax.optimization_barrier((query_t, part))
            if s:
                got[half].append(wide(xor_permute(narrow(part), n, CORES * s)))
            elif half == 0:
                part = combine(part, got[0], True)
                across.append(wide(xor_permute(narrow(part), n, n_patch)))
            else:
                part = combine(part, got[1], False)
                mine, *sent = scatter(at, part, across)
    far_got = {}
    for s in sorted(range(1, n_far), key=lambda s: (-s.bit_length(), s)):
        far_got[s] = wide(xor_permute(narrow(sent[s - 1]), n, n_patch * NEAR * s))
    pieces = [attended(mine, [far_got[s] for s in range(1, n_far)])]
    pieces += [xor_permute(pieces[0], n, CORES * s) for s in range(1, n_x)]
    pieces = [p for piece in pieces for p in (piece, xor_permute(piece, n, 1))]
    return finish(at, pieces, w_out)


def solution(mesh):
    return jax.shard_map(
        functools.partial(per_device, mesh.shape["tm"], mesh.shape["patch"]),
        mesh=mesh,
        in_specs=(P(), P(("tm", "patch"), None), P(), P(), P(), P(None, "patch")),
        out_specs=P("tm", "patch"),
        check_vma=False,
    )
```

```python
import functools
import math

import jax
import jax.numpy as jnp
from jax import lax
from jax.experimental import pallas as pl
from jax.experimental.pallas import tpu as pltpu
from jax.sharding import PartitionSpec as P

H = 8
CORES = 2
NEAR = 2
AXES = ("tm", "patch")
VMEM = pl.BlockSpec(memory_space=pltpu.VMEM)
HBM = pl.BlockSpec(memory_space=pltpu.HBM)
SMEM = pl.BlockSpec(memory_space=pltpu.SMEM)
PARAMS = pltpu.CompilerParams(vmem_limit_bytes=24 * 2**20)
EXTRA = 8
LEVELS = 30.0 * 2.0**10
UNITS = (2.0**20, 2.0**10, 1.0, 2.0**-10, 2.0**-20)


def xor_permute(value, n, step):
    return lax.ppermute(value, AXES, [(i, i ^ step) for i in range(n)])


def dot(a, w):
    return jnp.dot(a, w, preferred_element_type=jnp.float32).astype(jnp.bfloat16)


def project_own_kernel(at_ref, t_hbm, l_hbm, wq_hbm, wk_hbm, wv_hbm, k_ref, v_ref, q_ref, wk_ref, wv_ref, wq_ref, t_ref, l_ref, sems):
    near, core = at_ref[1], at_ref[3]
    n = t_ref.shape[0]
    cols = k_ref.shape[1]
    size = cols // (H // CORES)
    coef = math.log2(math.e) / math.sqrt(size)
    half = l_ref.shape[1] * l_ref.shape[2]
    columns = pl.ds(pl.multiple_of(core * cols, cols), cols)
    parts = [slice(0, n // 4), slice(n // 4, n // 2), slice(n // 2, n)]
    moves = [(wk_hbm.at[:, columns], wk_ref), (t_hbm.at[parts[0]], t_ref.at[parts[0]])]
    moves += [(wv_hbm.at[:, columns], wv_ref)] + [(t_hbm.at[p], t_ref.at[p]) for p in parts[1:]]
    moves += [(wq_hbm.at[:, columns], wq_ref), (l_hbm.at[:, near ^ 1], l_ref.at[0]), (l_hbm.at[:, near], l_ref.at[1])]
    copies = [pltpu.make_async_copy(src, dst, sems.at[i]) for i, (src, dst) in enumerate(moves)]

    def wait(*which):
        for i in which:
            copies[i].wait()

    def project_keys(part):
        k_ref[part, :] = dot(t_ref[part, :], wk_ref[...])

    def project_vals(part):
        v_ref[:, part] = dot(t_ref[part, :], wv_ref[...]).T

    for copy in copies:
        copy.start()
    wait(0, 1)
    project_keys(parts[0])
    wait(2, 3)
    project_vals(parts[0])
    project_keys(parts[1])
    project_vals(parts[1])
    wait(4)
    project_keys(parts[2])
    project_vals(parts[2])
    wait(5, 6, 7)
    for h in range(NEAR):
        query = dot(l_ref[h].reshape(half, -1), wq_ref[...]).T.astype(jnp.float32) * coef
        high = query.astype(jnp.bfloat16)
        low = (query - high.astype(jnp.float32)).astype(jnp.bfloat16)
        for j in range(cols // size):
            rows = slice(j * size, (j + 1) * size)
            q_ref[2 * j * size : (2 * j + 1) * size, h * half : (h + 1) * half] = high[rows]
            q_ref[(2 * j + 1) * size : (2 * j + 2) * size, h * half : (h + 1) * half] = low[rows]


def project_own(at, tokens, latents, w_query, w_key, w_value):
    (n, d), cols = tokens.shape, w_key.shape[1] // CORES
    n_far, _, block, _ = latents.shape
    m = n_far * NEAR * block
    return pl.pallas_call(
        project_own_kernel,
        out_shape=[jax.ShapeDtypeStruct(s, jnp.bfloat16) for s in ((n, cols), (cols, n), (2 * cols, m), (d, cols), (d, cols))],
        in_specs=[SMEM] + [HBM] * 5,
        out_specs=[VMEM] * 5,
        scratch_shapes=[
            pltpu.VMEM((d, cols), jnp.bfloat16),
            pltpu.VMEM((n, d), jnp.bfloat16),
            pltpu.VMEM((NEAR, n_far, block, d), jnp.bfloat16),
            pltpu.SemaphoreType.DMA((8,)),
        ],
        compiler_params=pltpu.CompilerParams(vmem_limit_bytes=45 * 2**20),
        cost_estimate=pl.CostEstimate(
            flops=(4 * n + 2 * m) * d * cols, bytes_accessed=2 * (n * d + m * d + 3 * d * cols), transcendentals=0
        ),
    )(at, tokens, latents, w_query, w_key, w_value)


def project_kernel(t_hbm, wk_ref, wv_ref, k_ref, v_ref, t_ref, sems):
    n = t_ref.shape[0]
    parts = [slice(0, n // 4), slice(n // 4, n // 2), slice(n // 2, n)]
    copies = [pltpu.make_async_copy(t_hbm.at[p], t_ref.at[p], sems.at[i]) for i, p in enumerate(parts)]
    for copy in copies:
        copy.start()
    for copy, part in zip(copies, parts):
        copy.wait()
        k_ref[part, :] = dot(t_ref[part, :], wk_ref[...])
        v_ref[:, part] = dot(t_ref[part, :], wv_ref[...]).T


def project(tokens, w_key, w_value):
    (n, d), cols = tokens.shape, w_key.shape[1]
    return pl.pallas_call(
        project_kernel,
        out_shape=[jax.ShapeDtypeStruct(s, jnp.bfloat16) for s in ((n, cols), (cols, n))],
        in_specs=[HBM, VMEM, VMEM],
        out_specs=[VMEM] * 2,
        scratch_shapes=[pltpu.VMEM((n, d), jnp.bfloat16), pltpu.SemaphoreType.DMA((3,))],
        compiler_params=PARAMS,
        cost_estimate=pl.CostEstimate(flops=4 * n * d * cols, bytes_accessed=2 * (n * d + 2 * d * cols), transcendentals=0),
    )(tokens, w_key, w_value)


def merge(parts):
    peak = functools.reduce(jnp.maximum, [p for _, _, p in parts])
    factors = [jnp.exp2(p - peak) for _, _, p in parts]
    num, den = (
        functools.reduce(lambda a, b: a + b, [part[i] * f for part, f in zip(parts, factors)]) for i in range(2)
    )
    return num, den, peak


def nearest(value):
    return jnp.floor(value + 0.5)


def spread(value):
    place = nearest(jnp.abs(value) * LEVELS) * 2.0**-10
    power = jnp.floor(place)
    return jnp.where(value < 0, -1.0, 1.0) * (1.0 + place - power) * jnp.exp2(power - 14.0)


def gather_up(value):
    size = jnp.abs(value)
    power = jnp.clip(jnp.floor(jnp.log2(size)), -14.0, 15.0)
    return jnp.where(value < 0, -1.0, 1.0) * (power + 13.0 + size * jnp.exp2(-power)) * (2.0**10 / LEVELS)


def encode(part):
    num, den, peak = part
    mean = num / den
    most = jnp.max(jnp.abs(mean), axis=0, keepdims=True)
    exponent = jnp.ceil(jnp.log2(jnp.clip(most, 2.0**-100, 2.0**100)) + 2.0**-10)
    rest, digits = peak + jnp.log2(den), [exponent]
    for unit in UNITS[:-1]:
        digits.append(nearest(rest * (1.0 / unit)))
        rest = rest - digits[-1] * unit
    digits.append(rest * (1.0 / UNITS[-1]))
    row = lax.broadcasted_iota(jnp.int32, (EXTRA, mean.shape[1]), 0)
    tail = jnp.zeros((EXTRA, mean.shape[1]), jnp.float32)
    for i, digit in enumerate(digits):
        tail = jnp.where(row == i, digit, tail)
    return jnp.concatenate([spread(mean * jnp.exp2(-exponent)), tail], axis=0)


def decode(rows):
    feats = rows.shape[0] - EXTRA
    exponent, *digits = (rows[feats + i : feats + i + 1] for i in range(len(UNITS) + 1))
    peak = functools.reduce(lambda a, b: a + b, [d * u for d, u in zip(reversed(digits), reversed(UNITS))])
    return gather_up(rows[:feats]) * jnp.exp2(exponent), jnp.ones_like(peak), peak


def unpack(rows):
    feats = rows.shape[0] - EXTRA
    return rows[:feats], rows[feats : feats + 1], rows[feats + 1 : feats + 2]


def pack(part):
    num, den, peak = part
    row = lax.broadcasted_iota(jnp.int32, (EXTRA, num.shape[1]), 0)
    return jnp.concatenate([num, jnp.where(row == 0, den, peak)], axis=0)


def attend_kernel(chunk, half, blocks, encoded, at_ref, q_ref, *refs):
    kv, got, (o_ref, s0, s1) = refs[: 2 * blocks], refs[2 * blocks : -3], refs[-3:]
    tokens, lanes = s0.shape
    heads, n_far, rows, block = o_ref.shape
    size = rows - EXTRA
    slots = (s0, s1)
    ones = jnp.ones((16, chunk), jnp.bfloat16)
    items = [(j, b) for j in range(heads) for b in range(blocks)]

    def columns(j):
        return pl.ds(pl.multiple_of((at_ref[0] * heads + j) * size, size), size)

    peak, done = None, []
    for i in range(len(items) + 1):
        now, before = slots[i % 2], slots[(i - 1) % 2]
        acc, top = jnp.zeros((size + 16, lanes), jnp.float32), None
        for c in range(tokens // chunk):
            part = slice(c * chunk, (c + 1) * chunk)
            if i < len(items):
                j, b = items[i]
                q = q_ref[pl.ds(pl.multiple_of((at_ref[0] * heads + j) * 2 * size, 2 * size), 2 * size), half * lanes : (half + 1) * lanes]
                k = kv[2 * b][part, columns(j)]
                s = jnp.dot(jnp.concatenate([k, k], axis=1), q, preferred_element_type=jnp.float32)
                now[part, :] = s
                high = jnp.max(s.reshape(chunk // 8, 8, lanes), axis=0)
                top = high if top is None else jnp.maximum(top, high)
            if i > 0:
                j, b = items[i - 1]
                w = jnp.exp2(before[part, :] - peak).astype(jnp.bfloat16)
                v = jnp.concatenate([kv[2 * b + 1][columns(j), part], ones], axis=0)
                acc = acc + jnp.dot(v, w, preferred_element_type=jnp.float32)
        if i > 0:
            j = items[i - 1][0]
            done.append((acc[:size], acc[size : size + 1], peak))
            if len(done) == blocks:
                for f in range(n_far):
                    at = slice(f * block, (f + 1) * block)
                    part = merge([tuple(v[:, at] for v in d) for d in done] + [unpack(g[j, f]) for g in got])
                    o_ref[j, f] = encode(part) if encoded else pack(part)
                done = []
        if i < len(items):
            peak = jnp.max(top, axis=0, keepdims=True)


def attend(group, half, query_t, blocks, got, shape, encoded, chunk=1024):
    heads, n_far, rows, block = shape
    lanes, tokens = n_far * block, blocks[0][0].shape[0]
    return pl.pallas_call(
        functools.partial(attend_kernel, chunk, half, len(blocks), encoded),
        out_shape=jax.ShapeDtypeStruct(shape, jnp.float32),
        in_specs=[SMEM] + [VMEM] * (1 + 2 * len(blocks) + len(got)),
        out_specs=VMEM,
        scratch_shapes=[pltpu.VMEM((tokens, lanes), jnp.float32)] * 2,
        compiler_params=PARAMS,
        cost_estimate=pl.CostEstimate(
            flops=4 * tokens * lanes * (rows - EXTRA) * heads * len(blocks),
            bytes_accessed=4 * math.prod(shape),
            transcendentals=tokens * lanes * heads * len(blocks),
        ),
    )(group.astype(jnp.int32).reshape(1), query_t, *[a for pair in blocks for a in pair], *got)


def combine_kernel(encoded, own_ref, *refs):
    got, out = refs[:-1], refs[-1]
    heads, n_far = own_ref.shape[:2]
    for j in range(heads):
        for f in range(n_far):
            part = merge([unpack(own_ref[j, f])] + [decode(g[j, f]) for g in got])
            out[j, f] = encode(part) if encoded else pack(part)


def combine(own, got, encoded):
    return pl.pallas_call(
        functools.partial(combine_kernel, encoded),
        out_shape=jax.ShapeDtypeStruct(own.shape, jnp.float32),
        in_specs=[VMEM] * (1 + len(got)),
        out_specs=VMEM,
        compiler_params=PARAMS,
        cost_estimate=pl.CostEstimate(flops=own.size * 20, bytes_accessed=own.size * 12, transcendentals=0),
    )(own, *got)


def scatter_kernel(n_far, at_ref, own_ref, *refs):
    got, outs = refs[:-n_far], refs[-n_far:]
    far = at_ref[4]
    for s, out in enumerate(outs):
        for j in range(own_ref.shape[0]):
            part = merge([unpack(own_ref[j, far ^ s])] + [decode(g[j, far ^ s]) for g in got])
            out[j] = encode(part) if s else pack(part)


def scatter(at, own, got):
    heads, n_far, rows, block = own.shape
    return pl.pallas_call(
        functools.partial(scatter_kernel, n_far),
        out_shape=[jax.ShapeDtypeStruct((heads, rows, block), jnp.float32)] * n_far,
        in_specs=[SMEM] + [VMEM] * (1 + len(got)),
        out_specs=[VMEM] * n_far,
        compiler_params=PARAMS,
        cost_estimate=pl.CostEstimate(flops=own.size * 20, bytes_accessed=own.size * 12, transcendentals=0),
    )(at, own, *got)


def attended_kernel(own_ref, *refs):
    got, out = refs[:-1], refs[-1]
    heads, rows, _ = own_ref.shape
    feats = rows - EXTRA
    for i in range(heads):
        num, den, _ = merge([unpack(own_ref[i])] + [decode(g[i]) for g in got])
        out[i * feats : (i + 1) * feats, :] = num / den


def attended(own, got):
    heads, rows, block = own.shape
    return pl.pallas_call(
        attended_kernel,
        out_shape=jax.ShapeDtypeStruct(((rows - EXTRA) * heads, block), jnp.float32),
        in_specs=[VMEM] * (1 + len(got)),
        out_specs=VMEM,
        compiler_params=PARAMS,
        cost_estimate=pl.CostEstimate(flops=own.size * 20, bytes_accessed=own.size * 16, transcendentals=0),
    )(own, *got)


def finish_kernel(at_ref, *refs):
    pieces, (w_ref, o_ref, normed) = refs[:-3], refs[-3:]
    feats, me = pieces[0].shape[0], at_ref[2]
    width = feats * len(pieces)
    squares = functools.reduce(lambda a, b: a + b, [jnp.square(p[...]) for p in pieces])
    scale = lax.rsqrt(jnp.sum(squares, axis=0, keepdims=True) * (1.0 / width) + 1e-06)
    for s, piece in enumerate(pieces):
        owner = me ^ s
        at = owner % CORES * (width // CORES) + owner // CORES * feats
        normed[pl.ds(pl.multiple_of(at, feats), feats), :] = (piece[...] * scale).astype(jnp.bfloat16)
    o_ref[...] = lax.dot_general(
        normed[...], w_ref[...], (((0,), (0,)), ((), ())), preferred_element_type=jnp.float32
    ).astype(jnp.bfloat16)


def finish(at, pieces, w_out):
    block = pieces[0].shape[1]
    return pl.pallas_call(
        finish_kernel,
        out_shape=jax.ShapeDtypeStruct((block, w_out.shape[1]), jnp.bfloat16),
        in_specs=[SMEM] + [VMEM] * (len(pieces) + 1),
        out_specs=VMEM,
        scratch_shapes=[pltpu.VMEM((w_out.shape[0], block), jnp.bfloat16)],
        compiler_params=PARAMS,
        cost_estimate=pl.CostEstimate(flops=2 * block * w_out.size, bytes_accessed=2 * w_out.size, transcendentals=0),
    )(at, *pieces, w_out)


def narrow(part):
    return part.astype(jnp.float16)


def wide(part):
    return part.astype(jnp.float32)


def per_device(n_tm, n_patch, latents, tokens, w_query, w_key, w_value, w_out):
    n, n_x, n_far = n_tm * n_patch, n_patch // CORES, n_tm // NEAR
    tm, patch = lax.axis_index("tm"), lax.axis_index("patch")
    x, core = patch // CORES, patch % CORES
    at = jnp.stack([x, tm % NEAR, patch, core, tm // NEAR]).astype(jnp.int32)
    heads = H // n_patch
    block, d = latents.shape[0] // n_tm, latents.shape[1]
    shape = (heads, n_far, d // H + EXTRA, block)

    sibling = xor_permute(tokens, n, 1)
    latents = latents.reshape(n_far, NEAR, block, d)
    keys, vals_t, query_t, own_key, own_value = project_own(at, tokens, latents, w_query, w_key, w_value)
    near = [(keys, vals_t)]
    both = None
    got, across = [[], []], []
    for s in range(n_x - 1, -1, -1):
        group = x ^ s
        for half in range(2):
            if both is None:
                part = attend(group, half, query_t, near, [], shape, False)
                sibling, part = lax.optimization_barrier((sibling, part))
                far = [tuple(project(sibling, own_key, own_value))]
                both = near + far
                part = attend(group, half, query_t, far, [part], shape, True)
            else:
                part = attend(group, half, query_t, both, [], shape, s > 0)
            query_t, part = lax.optimization_barrier((query_t, part))
            if s:
                got[half].append(wide(xor_permute(narrow(part), n, CORES * s)))
            elif half == 0:
                part = combine(part, got[0], True)
                across.append(wide(xor_permute(narrow(part), n, n_patch)))
            else:
                part = combine(part, got[1], False)
                mine, *sent = scatter(at, part, across)
    far_got = {}
    for s in sorted(range(1, n_far), key=lambda s: (-s.bit_length(), s)):
        far_got[s] = wide(xor_permute(narrow(sent[s - 1]), n, n_patch * NEAR * s))
    pieces = [attended(mine, [far_got[s] for s in range(1, n_far)])]
    pieces += [xor_permute(pieces[0], n, CORES * s) for s in range(1, n_x)]
    pieces = [p for piece in pieces for p in (piece, xor_permute(piece, n, 1))]
    return finish(at, pieces, w_out)


def solution(mesh):
    return jax.shard_map(
        functools.partial(per_device, mesh.shape["tm"], mesh.shape["patch"]),
        mesh=mesh,
        in_specs=(P(), P(("tm", "patch"), None), P(), P(), P(), P(None, "patch")),
        out_specs=P("tm", "patch"),
        check_vma=False,
    )
```

```python
import functools
import math

import jax
import jax.numpy as jnp
from jax import lax
from jax.experimental import pallas as pl
from jax.experimental.pallas import tpu as pltpu
from jax.sharding import PartitionSpec as P

H = 8
CORES = 2
NEAR = 2
AXES = ("tm", "patch")
VMEM = pl.BlockSpec(memory_space=pltpu.VMEM)
HBM = pl.BlockSpec(memory_space=pltpu.HBM)
SMEM = pl.BlockSpec(memory_space=pltpu.SMEM)
PARAMS = pltpu.CompilerParams(vmem_limit_bytes=24 * 2**20)
EXTRA = 8
LEVELS = 30.0 * 2.0**10
UNITS = (2.0**20, 2.0**10, 1.0, 2.0**-10, 2.0**-20)


def xor_permute(value, n, step):
    return lax.ppermute(value, AXES, [(i, i ^ step) for i in range(n)])


def dot(a, w):
    return jnp.dot(a, w, preferred_element_type=jnp.float32).astype(jnp.bfloat16)


def project_own_kernel(at_ref, t_hbm, l_hbm, wq_hbm, wk_hbm, wv_hbm, k_ref, v_ref, q_ref, wk_ref, wv_ref, wq_ref, t_ref, l_ref, sems):
    near, core = at_ref[1], at_ref[3]
    n = t_ref.shape[0]
    cols = k_ref.shape[1]
    half = l_ref.shape[1] * l_ref.shape[2]
    columns = pl.ds(pl.multiple_of(core * cols, cols), cols)
    parts = [slice(0, n // 4), slice(n // 4, n // 2), slice(n // 2, n)]
    moves = [(wk_hbm.at[:, columns], wk_ref), (t_hbm.at[parts[0]], t_ref.at[parts[0]])]
    moves += [(wv_hbm.at[:, columns], wv_ref)] + [(t_hbm.at[p], t_ref.at[p]) for p in parts[1:]]
    moves += [(wq_hbm.at[:, columns], wq_ref), (l_hbm.at[:, near ^ 1], l_ref.at[0]), (l_hbm.at[:, near], l_ref.at[1])]
    copies = [pltpu.make_async_copy(src, dst, sems.at[i]) for i, (src, dst) in enumerate(moves)]

    def wait(*which):
        for i in which:
            copies[i].wait()

    def project_keys(part):
        k_ref[part, :] = dot(t_ref[part, :], wk_ref[...])

    def project_vals(part):
        v_ref[:, part] = dot(t_ref[part, :], wv_ref[...]).T

    for copy in copies:
        copy.start()
    wait(0, 1)
    project_keys(parts[0])
    wait(2, 3)
    project_vals(parts[0])
    project_keys(parts[1])
    project_vals(parts[1])
    wait(4)
    project_keys(parts[2])
    project_vals(parts[2])
    wait(5, 6, 7)
    for h in range(NEAR):
        q_ref[:, h * half : (h + 1) * half] = dot(l_ref[h].reshape(half, -1), wq_ref[...]).T


def project_own(at, tokens, latents, w_query, w_key, w_value):
    (n, d), cols = tokens.shape, w_key.shape[1] // CORES
    n_far, _, block, _ = latents.shape
    m = n_far * NEAR * block
    return pl.pallas_call(
        project_own_kernel,
        out_shape=[jax.ShapeDtypeStruct(s, jnp.bfloat16) for s in ((n, cols), (cols, n), (cols, m), (d, cols), (d, cols))],
        in_specs=[SMEM] + [HBM] * 5,
        out_specs=[VMEM] * 5,
        scratch_shapes=[
            pltpu.VMEM((d, cols), jnp.bfloat16),
            pltpu.VMEM((n, d), jnp.bfloat16),
            pltpu.VMEM((NEAR, n_far, block, d), jnp.bfloat16),
            pltpu.SemaphoreType.DMA((8,)),
        ],
        compiler_params=pltpu.CompilerParams(vmem_limit_bytes=46 * 2**20),
        cost_estimate=pl.CostEstimate(
            flops=(4 * n + 2 * m) * d * cols, bytes_accessed=2 * (n * d + m * d + 3 * d * cols), transcendentals=0
        ),
    )(at, tokens, latents, w_query, w_key, w_value)


def project_kernel(t_hbm, wk_ref, wv_ref, k_ref, v_ref, t_ref, sems):
    n = t_ref.shape[0]
    parts = [slice(0, n // 4), slice(n // 4, n // 2), slice(n // 2, n)]
    copies = [pltpu.make_async_copy(t_hbm.at[p], t_ref.at[p], sems.at[i]) for i, p in enumerate(parts)]
    for copy in copies:
        copy.start()
    for copy, part in zip(copies, parts):
        copy.wait()
        k_ref[part, :] = dot(t_ref[part, :], wk_ref[...])
        v_ref[:, part] = dot(t_ref[part, :], wv_ref[...]).T


def project(tokens, w_key, w_value):
    (n, d), cols = tokens.shape, w_key.shape[1]
    return pl.pallas_call(
        project_kernel,
        out_shape=[jax.ShapeDtypeStruct(s, jnp.bfloat16) for s in ((n, cols), (cols, n))],
        in_specs=[HBM, VMEM, VMEM],
        out_specs=[VMEM] * 2,
        scratch_shapes=[pltpu.VMEM((n, d), jnp.bfloat16), pltpu.SemaphoreType.DMA((3,))],
        compiler_params=PARAMS,
        cost_estimate=pl.CostEstimate(flops=4 * n * d * cols, bytes_accessed=2 * (n * d + 2 * d * cols), transcendentals=0),
    )(tokens, w_key, w_value)


def merge(parts):
    peak = functools.reduce(jnp.maximum, [p for _, _, p in parts])
    factors = [jnp.exp2(p - peak) for _, _, p in parts]
    num, den = (
        functools.reduce(lambda a, b: a + b, [part[i] * f for part, f in zip(parts, factors)]) for i in range(2)
    )
    return num, den, peak


def nearest(value):
    return jnp.floor(value + 0.5)


def spread(value):
    place = nearest(jnp.abs(value) * LEVELS) * 2.0**-10
    power = jnp.floor(place)
    return jnp.where(value < 0, -1.0, 1.0) * (1.0 + place - power) * jnp.exp2(power - 14.0)


def gather_up(value):
    size = jnp.abs(value)
    power = jnp.clip(jnp.floor(jnp.log2(size)), -14.0, 15.0)
    return jnp.where(value < 0, -1.0, 1.0) * (power + 13.0 + size * jnp.exp2(-power)) * (2.0**10 / LEVELS)


def encode(part):
    num, den, peak = part
    mean = num / den
    most = jnp.max(jnp.abs(mean), axis=0, keepdims=True)
    exponent = jnp.ceil(jnp.log2(jnp.clip(most, 2.0**-100, 2.0**100)) + 2.0**-10)
    rest, digits = peak + jnp.log2(den), [exponent]
    for unit in UNITS[:-1]:
        digits.append(nearest(rest * (1.0 / unit)))
        rest = rest - digits[-1] * unit
    digits.append(rest * (1.0 / UNITS[-1]))
    row = lax.broadcasted_iota(jnp.int32, (EXTRA, mean.shape[1]), 0)
    tail = jnp.zeros((EXTRA, mean.shape[1]), jnp.float32)
    for i, digit in enumerate(digits):
        tail = jnp.where(row == i, digit, tail)
    return jnp.concatenate([spread(mean * jnp.exp2(-exponent)), tail], axis=0)


def decode(rows):
    feats = rows.shape[0] - EXTRA
    exponent, *digits = (rows[feats + i : feats + i + 1] for i in range(len(UNITS) + 1))
    peak = functools.reduce(lambda a, b: a + b, [d * u for d, u in zip(reversed(digits), reversed(UNITS))])
    return gather_up(rows[:feats]) * jnp.exp2(exponent), jnp.ones_like(peak), peak


def unpack(rows):
    feats = rows.shape[0] - EXTRA
    return rows[:feats], rows[feats : feats + 1], rows[feats + 1 : feats + 2]


def pack(part):
    num, den, peak = part
    row = lax.broadcasted_iota(jnp.int32, (EXTRA, num.shape[1]), 0)
    return jnp.concatenate([num, jnp.where(row == 0, den, peak)], axis=0)


def attend_kernel(chunk, half, blocks, encoded, at_ref, q_ref, *refs):
    kv, got, (o_ref, s0, s1) = refs[: 2 * blocks], refs[2 * blocks : -3], refs[-3:]
    tokens, lanes = s0.shape
    heads, n_far, rows, block = o_ref.shape
    size = rows - EXTRA
    coef = math.log2(math.e) / math.sqrt(size)
    slots = (s0, s1)
    ones = jnp.ones((16, chunk), jnp.bfloat16)
    items = [(j, b) for j in range(heads) for b in range(blocks)]

    def columns(j):
        return pl.ds(pl.multiple_of((at_ref[0] * heads + j) * size, size), size)

    peak, done = None, []
    for i in range(len(items) + 1):
        now, before = slots[i % 2], slots[(i - 1) % 2]
        acc, top = jnp.zeros((size + 16, lanes), jnp.float32), None
        for c in range(tokens // chunk):
            part = slice(c * chunk, (c + 1) * chunk)
            if i < len(items):
                j, b = items[i]
                q = q_ref[columns(j), half * lanes : (half + 1) * lanes]
                s = jnp.dot(kv[2 * b][part, columns(j)], q, preferred_element_type=jnp.float32)
                now[part, :] = s
                high = jnp.max(s.reshape(chunk // 8, 8, lanes), axis=0)
                top = high if top is None else jnp.maximum(top, high)
            if i > 0:
                j, b = items[i - 1]
                w = jnp.exp2((before[part, :] - peak) * coef).astype(jnp.bfloat16)
                v = jnp.concatenate([kv[2 * b + 1][columns(j), part], ones], axis=0)
                acc = acc + jnp.dot(v, w, preferred_element_type=jnp.float32)
        if i > 0:
            j = items[i - 1][0]
            done.append((acc[:size], acc[size : size + 1], peak * coef))
            if len(done) == blocks:
                for f in range(n_far):
                    at = slice(f * block, (f + 1) * block)
                    part = merge([tuple(v[:, at] for v in d) for d in done] + [unpack(g[j, f]) for g in got])
                    o_ref[j, f] = encode(part) if encoded else pack(part)
                done = []
        if i < len(items):
            peak = jnp.max(top, axis=0, keepdims=True)


def attend(group, half, query_t, blocks, got, shape, encoded, chunk=1024):
    heads, n_far, rows, block = shape
    lanes, tokens = n_far * block, blocks[0][0].shape[0]
    return pl.pallas_call(
        functools.partial(attend_kernel, chunk, half, len(blocks), encoded),
        out_shape=jax.ShapeDtypeStruct(shape, jnp.float32),
        in_specs=[SMEM] + [VMEM] * (1 + 2 * len(blocks) + len(got)),
        out_specs=VMEM,
        scratch_shapes=[pltpu.VMEM((tokens, lanes), jnp.float32)] * 2,
        compiler_params=PARAMS,
        cost_estimate=pl.CostEstimate(
            flops=4 * tokens * lanes * (rows - EXTRA) * heads * len(blocks),
            bytes_accessed=4 * math.prod(shape),
            transcendentals=tokens * lanes * heads * len(blocks),
        ),
    )(group.astype(jnp.int32).reshape(1), query_t, *[a for pair in blocks for a in pair], *got)


def combine_kernel(encoded, own_ref, *refs):
    got, out = refs[:-1], refs[-1]
    heads, n_far = own_ref.shape[:2]
    for j in range(heads):
        for f in range(n_far):
            part = merge([unpack(own_ref[j, f])] + [decode(g[j, f]) for g in got])
            out[j, f] = encode(part) if encoded else pack(part)


def combine(own, got, encoded):
    return pl.pallas_call(
        functools.partial(combine_kernel, encoded),
        out_shape=jax.ShapeDtypeStruct(own.shape, jnp.float32),
        in_specs=[VMEM] * (1 + len(got)),
        out_specs=VMEM,
        compiler_params=PARAMS,
        cost_estimate=pl.CostEstimate(flops=own.size * 20, bytes_accessed=own.size * 12, transcendentals=0),
    )(own, *got)


def scatter_kernel(n_far, at_ref, own_ref, *refs):
    got, outs = refs[:-n_far], refs[-n_far:]
    far = at_ref[4]
    for s, out in enumerate(outs):
        for j in range(own_ref.shape[0]):
            part = merge([unpack(own_ref[j, far ^ s])] + [decode(g[j, far ^ s]) for g in got])
            out[j] = encode(part) if s else pack(part)


def scatter(at, own, got):
    heads, n_far, rows, block = own.shape
    return pl.pallas_call(
        functools.partial(scatter_kernel, n_far),
        out_shape=[jax.ShapeDtypeStruct((heads, rows, block), jnp.float32)] * n_far,
        in_specs=[SMEM] + [VMEM] * (1 + len(got)),
        out_specs=[VMEM] * n_far,
        compiler_params=PARAMS,
        cost_estimate=pl.CostEstimate(flops=own.size * 20, bytes_accessed=own.size * 12, transcendentals=0),
    )(at, own, *got)


def attended_kernel(own_ref, *refs):
    got, out = refs[:-1], refs[-1]
    heads, rows, _ = own_ref.shape
    feats = rows - EXTRA
    for i in range(heads):
        num, den, _ = merge([unpack(own_ref[i])] + [decode(g[i]) for g in got])
        out[i * feats : (i + 1) * feats, :] = num / den


def attended(own, got):
    heads, rows, block = own.shape
    return pl.pallas_call(
        attended_kernel,
        out_shape=jax.ShapeDtypeStruct(((rows - EXTRA) * heads, block), jnp.float32),
        in_specs=[VMEM] * (1 + len(got)),
        out_specs=VMEM,
        compiler_params=PARAMS,
        cost_estimate=pl.CostEstimate(flops=own.size * 20, bytes_accessed=own.size * 16, transcendentals=0),
    )(own, *got)


def finish_kernel(at_ref, *refs):
    pieces, (w_ref, o_ref) = refs[:-2], refs[-2:]
    feats, me = pieces[0].shape[0], at_ref[2]
    width = feats * len(pieces)
    squares = functools.reduce(lambda a, b: a + b, [jnp.square(p[...]) for p in pieces])
    scale = lax.rsqrt(jnp.sum(squares, axis=0, keepdims=True) * (1.0 / width) + 1e-06)
    out = jnp.zeros(o_ref.shape, jnp.float32)
    for s, piece in enumerate(pieces):
        owner = me ^ s
        at = owner % CORES * (width // CORES) + owner // CORES * feats
        normed = (piece[...] * scale).astype(jnp.bfloat16)
        rows = w_ref[pl.ds(pl.multiple_of(at, feats), feats), :]
        out = out + lax.dot_general(normed, rows, (((0,), (0,)), ((), ())), preferred_element_type=jnp.float32)
    o_ref[...] = out.astype(jnp.bfloat16)


def finish(at, pieces, w_out):
    block = pieces[0].shape[1]
    return pl.pallas_call(
        finish_kernel,
        out_shape=jax.ShapeDtypeStruct((block, w_out.shape[1]), jnp.bfloat16),
        in_specs=[SMEM] + [VMEM] * (len(pieces) + 1),
        out_specs=VMEM,
        compiler_params=PARAMS,
        cost_estimate=pl.CostEstimate(flops=2 * block * w_out.size, bytes_accessed=2 * w_out.size, transcendentals=0),
    )(at, *pieces, w_out)


def narrow(part):
    return part.astype(jnp.float16)


def wide(part):
    return part.astype(jnp.float32)


def per_device(n_tm, n_patch, latents, tokens, w_query, w_key, w_value, w_out):
    n, n_x, n_far = n_tm * n_patch, n_patch // CORES, n_tm // NEAR
    tm, patch = lax.axis_index("tm"), lax.axis_index("patch")
    x, core = patch // CORES, patch % CORES
    at = jnp.stack([x, tm % NEAR, patch, core, tm // NEAR]).astype(jnp.int32)
    heads = H // n_patch
    block, d = latents.shape[0] // n_tm, latents.shape[1]
    shape = (heads, n_far, d // H + EXTRA, block)

    sibling = xor_permute(tokens, n, 1)
    latents = latents.reshape(n_far, NEAR, block, d)
    keys, vals_t, query_t, own_key, own_value = project_own(at, tokens, latents, w_query, w_key, w_value)
    near = [(keys, vals_t)]
    both = None
    got, across = [[], []], []
    for s in range(n_x - 1, -1, -1):
        group = x ^ s
        for half in range(2):
            if both is None:
                part = attend(group, half, query_t, near, [], shape, False)
                sibling, part = lax.optimization_barrier((sibling, part))
                far = [tuple(project(sibling, own_key, own_value))]
                both = near + far
                part = attend(group, half, query_t, far, [part], shape, True)
            else:
                part = attend(group, half, query_t, both, [], shape, s > 0)
            query_t, part = lax.optimization_barrier((query_t, part))
            if s:
                got[half].append(wide(xor_permute(narrow(part), n, CORES * s)))
            elif half == 0:
                part = combine(part, got[0], True)
                across.append(wide(xor_permute(narrow(part), n, n_patch)))
            else:
                part = combine(part, got[1], False)
                mine, *sent = scatter(at, part, across)
    far_got = {}
    for s in sorted(range(1, n_far), key=lambda s: (-s.bit_length(), s)):
        far_got[s] = wide(xor_permute(narrow(sent[s - 1]), n, n_patch * NEAR * s))
    pieces = [attended(mine, [far_got[s] for s in range(1, n_far)])]
    pieces += [xor_permute(pieces[0], n, CORES * s) for s in range(1, n_x)]
    pieces = [p for piece in pieces for p in (piece, xor_permute(piece, n, 1))]
    return finish(at, pieces, w_out)


def solution(mesh):
    return jax.shard_map(
        functools.partial(per_device, mesh.shape["tm"], mesh.shape["patch"]),
        mesh=mesh,
        in_specs=(P(), P(("tm", "patch"), None), P(), P(), P(), P(None, "patch")),
        out_specs=P("tm", "patch"),
        check_vma=False,
    )
```
